256 devices in a mesh: dom: 64 (over x, y_lo, z), rep: 4 (over y_hi, core).
Axes of the slice: x: 4, y: 4 (y_hi: 2, y_lo: 2; y = y_hi * 2 + y_lo), z: 8, core: 2. Of those that a mesh axis runs over, the one named last changes fastest.
Arguments:
- left_embedding: float32 [16384, 400], P('dom'), may hold values from -1.8 to 1.8
- left_state: float32 [16384], P('dom'), may hold values from 0.01 to 1
- right_embedding: float32 [16384, 400], P('dom'), may hold values from -1.8 to 1.8
- right_state: float32 [16384], P('dom'), may hold values from 0.01 to 1
- relation: float32 [1536, 400], replicated, may hold values from -4 to 4
- sources: int32 [64, 2048], P('dom', 'rep'), may hold values from 0 to 255
- relation_ids: int32 [64, 2048], P('dom', 'rep'), may hold values from 0 to 1535, as said below
- destinations: int32 [64, 2048], P('dom', 'rep'), may hold values from 0 to 255
- negatives_left: int32 [64, 4, 1000], P('dom', 'rep'), may hold values from 0 to 255
- negatives_right: int32 [64, 4, 1000], P('dom', 'rep'), may hold values from 0 to 255
- edge_counts: int32 [64], P('dom'), may hold values from 682 to 2048, as said below
Outputs:
- left_next: float32 [16384, 400], P('dom')
- left_state_next: float32 [16384], P('dom')
- right_next: float32 [16384, 400], P('dom')
- right_state_next: float32 [16384], P('dom')
- relation_grad: float32 [1536, 400], replicated
The draws below stay inside these ranges and needn't reach their ends.
Inputs may be any that keep to these rules, and one draw needn't show every extreme that they name: `relation_ids`: integers of 0 to 1535. The live edges of a bucket are its first edge_counts slots; some bucket is full.
All inputs are finite; a program needn't handle non-finite values.
Results may differ from the reference program's by a relative error of at most 0.0003.
Values sent between devices are 32-bit elements; how exact they have to be, the bound alone decides.
No kernel may reach another device: no remote copies, remote signals or barrier semaphores. Data moves between devices by JAX's collectives and lax.ppermute only.
A program may use at most 64 MiB of HBM per device.

```python
import math
import jax
import jax.numpy as jnp
from jax import lax

D = 400
NEG = 1000
BATCH = 512
ROWS = 256
BATCHES_DEV = 1
REL = 1536
E_DEV = 512
EDGE_CAP = 2048
ENTITIES = 16384
N_DOM = 64
N_REP = 4


def draw_relation_ids(key, part):
    key = jax.random.fold_in(key, 11)
    block_width = max(REL // (N_DOM * N_REP), 1)
    bucket_ids = jnp.arange(N_DOM, dtype=jnp.int32)[:, None]
    slot_ids = jnp.arange(EDGE_CAP, dtype=jnp.int32)[None, :]
    device_ids = bucket_ids * N_REP + slot_ids // E_DEV
    home_start = device_ids * REL // (N_DOM * N_REP)
    local_pick = jax.random.randint(jax.random.fold_in(key, 1), (N_DOM, EDGE_CAP), 0, block_width)
    spread_pick = jax.random.randint(jax.random.fold_in(key, 2), (N_DOM, EDGE_CAP), 0, REL)
    choose_home = jax.random.randint(jax.random.fold_in(key, 3), (N_DOM, EDGE_CAP), 0, 4)
    return jnp.where(choose_home < 3, (home_start + local_pick) % REL, spread_pick).astype(jnp.int32)


def draw_edge_counts(key, part):
    key = jax.random.fold_in(key, 23)
    drawn = jax.random.randint(jax.random.fold_in(key, 1), (N_DOM,), EDGE_CAP // 3, EDGE_CAP + 1)
    full_bucket = jax.random.randint(jax.random.fold_in(key, 2), (), 0, N_DOM)
    return jnp.where(jnp.arange(N_DOM, dtype=jnp.int32) == full_bucket, EDGE_CAP, drawn).astype(jnp.int32)


def set_ends(values, stream_key, low, top_value):
    longest = values.shape.index(max(values.shape))
    spots = []
    for shift in (0, 1):
        where = [jax.random.randint(jax.random.fold_in(stream_key, axis), (), 0, length) for axis, length in enumerate(values.shape)]
        where[longest] = (where[longest] + shift) % values.shape[longest]
        spots.append(tuple(where))
    return values.at[spots[0]].set(low).at[spots[1]].set(top_value)


def block_scale(key, shape, shards, least, top_value):
    level, own = 1.0, jax.random.fold_in(key, 6)
    for axis_at, shards_of in shards:
        steps = jnp.exp(jax.random.uniform(jax.random.fold_in(own, axis_at), (shards_of,), jnp.float32, least / len(shards), top_value / len(shards)))
        level = level * jnp.repeat(steps, shape[axis_at] // shards_of).reshape([-1 if axis == axis_at else 1 for axis in range(len(shape))])
    return level


def noise(rng, extent, width, most, cuts=(), held_as=jnp.bfloat16):
    array = width * jax.random.normal(rng, extent, jnp.float32)
    if cuts:
        array = array * block_scale(rng, extent, cuts, -0.22, 0.18)
    return jnp.clip(array, -most, most).astype(held_as)


def setup_inputs(seed: int = 0) -> dict:
    splits = jax.random.split(jax.random.key(seed), 12)
    return {
        "left_embedding": noise(splits[0], (ENTITIES, D), 0.3, 1.8, ((0, 64),), jnp.float32),
        "left_state": jnp.clip(jnp.exp(math.log(1.0) - 4.6051702 * jax.random.uniform(splits[1], (ENTITIES,), jnp.float32) ** block_scale(splits[1], (ENTITIES,), ((0, 64),), -0.2, 0.2)), 0.01, 1.0),
        "right_embedding": noise(splits[2], (ENTITIES, D), 0.3, 1.8, ((0, 64),), jnp.float32),
        "right_state": jnp.clip(jnp.exp(math.log(1.0) - 4.6051702 * jax.random.uniform(splits[3], (ENTITIES,), jnp.float32) ** block_scale(splits[3], (ENTITIES,), ((0, 64),), -0.2, 0.2)), 0.01, 1.0),
        "relation": noise(splits[4], (REL, D), 1.0, 4.0, (), jnp.float32),
        "sources": set_ends(jax.random.randint(splits[5], (N_DOM, EDGE_CAP), 0, ROWS), jax.random.fold_in(splits[5], 1), 0, ROWS - 1).astype(jnp.int32),
        "relation_ids": draw_relation_ids(jax.random.fold_in(splits[11], 71), 0),
        "destinations": set_ends(jax.random.randint(splits[7], (N_DOM, EDGE_CAP), 0, ROWS), jax.random.fold_in(splits[7], 1), 0, ROWS - 1).astype(jnp.int32),
        "negatives_left": set_ends(jax.random.randint(splits[8], (N_DOM, BATCHES_DEV * N_REP, NEG), 0, ROWS), jax.random.fold_in(splits[8], 1), 0, ROWS - 1).astype(jnp.int32),
        "negatives_right": set_ends(jax.random.randint(splits[9], (N_DOM, BATCHES_DEV * N_REP, NEG), 0, ROWS), jax.random.fold_in(splits[9], 1), 0, ROWS - 1).astype(jnp.int32),
        "edge_counts": draw_edge_counts(jax.random.fold_in(splits[11], 71), 0),
    }


MARGIN = 0.1
LEARN_RATE = 0.1
HIGHEST = lax.Precision.HIGHEST

def complex_product(vectors, weights):
    half_width = vectors.shape[-1] // 2
    vec_real, vec_imag = (vectors[:, :half_width], vectors[:, half_width:])
    weight_real, weight_imag = (weights[:, :half_width], weights[:, half_width:])
    return jnp.concatenate([vec_real * weight_real - vec_imag * weight_imag, vec_real * weight_imag + vec_imag * weight_real], axis=1)

def complex_adjoint(vectors, weights):
    half_width = vectors.shape[-1] // 2
    vec_real, vec_imag = (vectors[:, :half_width], vectors[:, half_width:])
    weight_real, weight_imag = (weights[:, :half_width], weights[:, half_width:])
    return jnp.concatenate([vec_real * weight_real + vec_imag * weight_imag, vec_imag * weight_real - vec_real * weight_imag], axis=1)

def batch_loss(left_rows, right_rows, relation, sources, relation_ids, destinations, negatives_left, negatives_right, edge_mask):
    weights = relation[relation_ids]
    targets = right_rows[destinations]
    queries = complex_product(left_rows[sources], weights)
    probes = complex_adjoint(targets, weights)
    positive = lax.optimization_barrier(jnp.sum(queries * targets, axis=1))
    contract = (((1,), (1,)), ((), ()))
    score_right = lax.dot_general(queries, right_rows[negatives_right], contract, precision=HIGHEST, preferred_element_type=jnp.float32)
    score_left = lax.dot_general(probes, left_rows[negatives_left], contract, precision=HIGHEST, preferred_element_type=jnp.float32)
    hinge_right = lax.optimization_barrier(jnp.mean(jax.nn.softplus(MARGIN - positive[:, None] + score_right), axis=1))
    hinge_left = lax.optimization_barrier(jnp.mean(jax.nn.softplus(MARGIN - positive[:, None] + score_left), axis=1))
    return jnp.sum((hinge_right + hinge_left) * edge_mask)

def adagrad_rows(embedding, state, gradient):
    new_state = state + lax.optimization_barrier(jnp.mean(gradient * gradient, axis=1))
    return (embedding - LEARN_RATE * gradient / jnp.sqrt(new_state)[:, None], new_state)

def reference(left_embedding, left_state, right_embedding, right_state, relation, sources, relation_ids, destinations, negatives_left, negatives_right, edge_counts):
    batch_total = BATCHES_DEV * N_REP
    stacked = (left_embedding.reshape(N_DOM, ROWS, D), left_state.reshape(N_DOM, ROWS), right_embedding.reshape(N_DOM, ROWS, D), right_state.reshape(N_DOM, ROWS), sources.reshape(N_DOM, batch_total, BATCH), relation_ids.reshape(N_DOM, batch_total, BATCH), destinations.reshape(N_DOM, batch_total, BATCH), negatives_left, negatives_right, edge_counts)

    def bucket_step(running, inputs):
        left_rows, left_sums, right_rows, right_sums, bucket_sources, bucket_relations, bucket_targets, bucket_negl, bucket_negr, bucket_count = inputs
        slot_ids = jnp.arange(EDGE_CAP, dtype=jnp.int32).reshape(batch_total, BATCH)
        edge_mask = (slot_ids < bucket_count).astype(jnp.float32)

        def total_loss(left_param, right_param, relation_param):
            loss_sum = jnp.zeros((), jnp.float32)
            for number in range(batch_total):
                loss_sum = loss_sum + batch_loss(left_param, right_param, relation_param, bucket_sources[number], bucket_relations[number], bucket_targets[number], bucket_negl[number], bucket_negr[number], edge_mask[number])
            return loss_sum
        loss_sum, pullback = jax.vjp(total_loss, left_rows, right_rows, relation)
        grad_left, grad_right, grad_relation = pullback(jnp.ones((), jnp.float32))
        new_left, new_left_sums = adagrad_rows(left_rows, left_sums, grad_left)
        new_right, new_right_sums = adagrad_rows(right_rows, right_sums, grad_right)
        return (running + grad_relation, (new_left, new_left_sums, new_right, new_right_sums))
    relation_grad, outputs = lax.scan(bucket_step, jnp.zeros((REL, D), jnp.float32), stacked)
    left_next = outputs[0].reshape(ENTITIES, D)
    left_state_next = outputs[1].reshape(ENTITIES)
    right_next = jnp.roll(outputs[2], -1, axis=0).reshape(ENTITIES, D)
    right_state_next = jnp.roll(outputs[3], -1, axis=0).reshape(ENTITIES)
    return (left_next, left_state_next, right_next, right_state_next, relation_grad)
```

```python
import jax
import jax.numpy as jnp
from jax import lax
from jax.sharding import PartitionSpec as P
from jax.experimental import pallas as pl
from jax.experimental.pallas import tpu as pltpu

MARGIN = 0.1
LEARN_RATE = 0.1
F32 = jnp.float32
BF16 = jnp.bfloat16
NN = (((1,), (0,)), ((), ()))
NT = (((1,), (1,)), ((), ()))


def parts(value):
    high = value.astype(BF16)
    return high, (value - high.astype(F32)).astype(BF16)


def dot(a, b, dims):
    return lax.dot_general(a, b, dims, preferred_element_type=F32)


def dot_picked(value, picks, dims):
    high, low = parts(value)
    return dot(high, picks, dims) + dot(low, picks, dims)


def dot_split(a, b, dims):
    return dot(a[0], b[0], dims) + (dot(a[0], b[1], dims) + dot(a[1], b[0], dims))


def product(v, w):
    return v[0] * w[0] - v[1] * w[1], v[0] * w[1] + v[1] * w[0]


def adjoint(v, w):
    return v[0] * w[0] + v[1] * w[1], v[1] * w[0] - v[0] * w[1]


def halves(x):
    half = x.shape[0] // 2
    return x[:half], x[half:]


def one_hot(ids, rows):
    return (lax.broadcasted_iota(jnp.int32, (rows, ids.shape[1]), 0) == ids).astype(F32)


CORES, X_SIZE, Y_SIZE, Z_SIZE = 2, 4, 4, 8
DEVICES = CORES * X_SIZE * Y_SIZE * Z_SIZE
LANES = 128
VMEM_LIMIT = 56 * 1024 * 1024


def place(dom, rep):
    return rep % 2, dom // 16, (rep // 2) * 2 + (dom // 8) % 2, dom % 8


def device(core, x, y, z):
    return ((x * 2 + y % 2) * 8 + z) * 4 + (y // 2) * 2 + core


def send(value, target):
    pairs = []
    for n in range(DEVICES):
        pairs.append((n, device(*target(*place(n // 4, n % 4)))))
    return lax.ppermute(value, ("dom", "rep"), pairs)


def to_core(value):
    return send(value, lambda core, x, y, z: (1 - core, x, y, z))


def to_x(value, step):
    return send(value, lambda core, x, y, z: (core, (x + step) % X_SIZE, y, z))


def to_y(value, step):
    return send(value, lambda core, x, y, z: (core, x, (y + step) % Y_SIZE, z))


def to_z(value, bit):
    return send(value, lambda core, x, y, z: (core, x, y, z ^ bit))


def to_bucket_before(value):
    pairs = []
    for n in range(DEVICES):
        pairs.append((n, (n - 4) % DEVICES))
    return lax.ppermute(value, ("dom", "rep"), pairs)


def piece_rows(total):
    block = total // LANES // (CORES * X_SIZE)
    piece = -(-block // (8 * Y_SIZE)) * 8
    return block, piece


def spans(width, types):
    block, piece = piece_rows(width * types)
    pad = piece * Y_SIZE - block
    found = []
    for k in range(types // LANES):
        row, end = k * width, (k + 1) * width
        while row < end:
            stop = min(end, (row // block + 1) * block)
            found.append((k, row - k * width, stop - row, row + (row // block) * pad))
            row = stop
    return found


def piece_at(half, x, y, r, s, piece):
    block = half * X_SIZE + (x + r) % X_SIZE
    return pl.multiple_of((block * Y_SIZE + (y + s) % Y_SIZE) * piece, 8)


def grad_kernel(place_ref, counts_ref, left_ref, right_ref, rel_ref, src_ref, rid_ref, dst_ref, negl_ref, negr_ref,
                rel_send_ref, rel_keep_ref, lr_send_ref, lr_keep_ref, rows_ref):
    slots = src_ref.shape[1]
    rows = left_ref.shape[1]
    types = rel_ref.shape[1]
    negatives = negl_ref.shape[1]
    left, right = left_ref[...], right_ref[...]
    left_parts, right_parts = parts(left), parts(right)
    pick_src = one_hot(src_ref[...], rows).astype(BF16)
    pick_dst = one_hot(dst_ref[...], rows).astype(BF16)
    pick_rel = one_hot(rid_ref[...], types).astype(BF16)
    source = dot(left_parts[0], pick_src, NN) + dot(left_parts[1], pick_src, NN)
    target = dot(right_parts[0], pick_dst, NN) + dot(right_parts[1], pick_dst, NN)
    weight = dot_picked(rel_ref[...], pick_rel, NN)
    s, t, w = halves(source), halves(target), halves(weight)
    q = jnp.concatenate(product(s, w), axis=0)
    p = jnp.concatenate(adjoint(t, w), axis=0)
    positive = jnp.sum(q * target, axis=0, keepdims=True)
    q_parts, p_parts = parts(q), parts(p)
    right_rows, left_rows = parts(right.T), parts(left.T)
    count_right = jnp.sum(one_hot(negr_ref[...], rows), axis=1, keepdims=True)
    count_left = jnp.sum(one_hot(negl_ref[...], rows), axis=1, keepdims=True)
    slot = lax.broadcasted_iota(jnp.int32, (1, slots), 1)
    live = (slot + place_ref[3] * slots < counts_ref[0]).astype(F32) * (1.0 / negatives)
    offset = MARGIN - positive
    g_right = jax.nn.sigmoid(offset + dot_split(right_rows, q_parts, NN)) * count_right * live
    g_left = jax.nn.sigmoid(offset + dot_split(left_rows, p_parts, NN)) * count_left * live
    d_pos = -(jnp.sum(g_right, axis=0, keepdims=True) + jnp.sum(g_left, axis=0, keepdims=True))
    gr_parts, gl_parts = parts(g_right), parts(g_left)
    d_q = dot_split(right_parts, gr_parts, NN) + d_pos * target
    d_p = dot_split(left_parts, gl_parts, NN)
    dq, dp = halves(d_q), halves(d_p)
    a, b = adjoint(dq, s), adjoint(dp, t)
    d_w = jnp.concatenate([a[0] + b[0], a[1] - b[1]], axis=0)
    d_relation = dot_picked(d_w, pick_rel, NT)
    width = d_relation.shape[0]
    core, x, y = place_ref[0], place_ref[1], place_ref[2]
    block, piece = piece_rows(width * types)
    pad = piece * Y_SIZE - block
    if pad:
        for k in range(CORES * X_SIZE):
            rows_ref[(k + 1) * (block + pad) - pad:(k + 1) * (block + pad), :] = jnp.zeros((pad, LANES), F32)
    for k, start, size, row in spans(width, types):
        rows_ref[row:row + size, :] = d_relation[start:start + size, k * LANES:(k + 1) * LANES]
    for out_ref, half in ((rel_send_ref, 1 - core), (rel_keep_ref, core)):
        for r in range(X_SIZE):
            for s in range(Y_SIZE):
                to = (r * Y_SIZE + s) * piece
                out_ref[to:to + piece, :] = rows_ref[pl.ds(piece_at(half, x, y, r, s, piece), piece), :]
    d_s = jnp.concatenate(adjoint(dq, w), axis=0)
    d_left = dot_split(p_parts, gl_parts, NT) + dot_picked(d_s, pick_src, NT)
    d_t = jnp.concatenate(product(dp, w), axis=0) + d_pos * q
    d_right = dot_split(q_parts, gr_parts, NT) + dot_picked(d_t, pick_dst, NT)
    first = core == 0
    half = rows // CORES
    for at, grad in ((0, d_left), (width, d_right)):
        low, high = grad[:, :half], grad[:, half:]
        lr_keep_ref[at:at + width, :] = jnp.where(first, low, high)
        lr_send_ref[at:at + width, :] = jnp.where(first, high, low)


SCALAR, WHOLE = pl.BlockSpec(memory_space=pltpu.SMEM), pl.BlockSpec(memory_space=pltpu.VMEM)


def call(kernel, scalars, arrays, shapes, scratch=()):
    return pl.pallas_call(
        kernel,
        out_shape=[jax.ShapeDtypeStruct(shape, F32) for shape in shapes],
        in_specs=[SCALAR] * len(scalars) + [WHOLE] * len(arrays),
        out_specs=[WHOLE] * len(shapes),
        scratch_shapes=[pltpu.VMEM(shape, F32) for shape in scratch],
        compiler_params=pltpu.CompilerParams(vmem_limit_bytes=VMEM_LIMIT),
    )(*scalars, *arrays)


def adagrad_kernel(place_ref, kept_ref, got_ref, left_ref, right_ref, left_state_ref, right_state_ref, new_left_ref, new_right_ref):
    width = left_ref.shape[0]
    first = place_ref[0] == 0
    for at, rows_ref, state_ref, out_ref in (
        (0, left_ref, left_state_ref, new_left_ref),
        (width, right_ref, right_state_ref, new_right_ref),
    ):
        half = rows_ref.shape[1] // CORES
        gradient = kept_ref[at:at + width, :] + got_ref[at:at + width, :]
        embedding = jnp.where(first, rows_ref[:, :half], rows_ref[:, half:])
        state = jnp.where(first, state_ref[:, :half], state_ref[:, half:])
        new_state = state + jnp.sum(gradient * gradient, axis=0, keepdims=True) * (1.0 / width)
        out_ref[:width, :] = embedding - gradient * (LEARN_RATE / jnp.sqrt(new_state))
        out_ref[width:, :] = jnp.broadcast_to(new_state, (8, half))


def join_kernel(place_ref, own_left_ref, other_left_ref, own_right_ref, other_right_ref, left_ref, left_state_ref, right_ref, right_state_ref):
    first = place_ref[0] == 0
    width = left_ref.shape[0]
    half = own_left_ref.shape[1]
    for own_ref, other_ref, rows_ref, state_ref in (
        (own_left_ref, other_left_ref, left_ref, left_state_ref),
        (own_right_ref, other_right_ref, right_ref, right_state_ref),
    ):
        own, other = own_ref[...], other_ref[...]
        for at, value in ((0, jnp.where(first, own, other)), (half, jnp.where(first, other, own))):
            rows_ref[:, at:at + half] = value[:width]
            state_ref[:, at:at + half] = value[width:width + 1]


def relation_kernel(place_ref, own_ref, other_ref, out_ref, rows_ref):
    core, x, y = place_ref[0], place_ref[1], place_ref[2]
    width, types = out_ref.shape
    piece = piece_rows(width * types)[1]
    for in_ref, half in ((own_ref, core), (other_ref, 1 - core)):
        for r in range(X_SIZE):
            for s in range(Y_SIZE):
                at = (r * Y_SIZE + s) * piece
                rows_ref[pl.ds(piece_at(half, x, y, r, s, piece), piece), :] = in_ref[at:at + piece, :]
    for k, start, size, row in spans(width, types):
        out_ref[start:start + size, k * LANES:(k + 1) * LANES] = rows_ref[row:row + size, :]


def scatter(pieces, move):
    return sum([move(pieces[r], r) for r in range(1, len(pieces))], pieces[0])


def gather(own, count, move):
    return jnp.concatenate([own] + [move(own, (count - r) % count) for r in range(1, count)], axis=0)


def body(left_embedding, left_state, right_embedding, right_state, relation, sources, relation_ids, destinations, negatives_left, negatives_right, edge_counts):
    left, right, relation = left_embedding.T, right_embedding.T, relation.T
    width, types = relation.shape
    rows = left.shape[1]
    rep = lax.axis_index("rep")
    core, x, y, _ = place(lax.axis_index("dom"), rep)
    where = jnp.stack([core, x, y, rep]).astype(jnp.int32)
    piece = piece_rows(width * types)[1]
    block = piece * Y_SIZE
    half = (block * X_SIZE, LANES)
    lr_half = (2 * width, rows // CORES)
    rel_send, rel_keep, lr_send, lr_keep = call(
        grad_kernel,
        [where, edge_counts],
        [left, right, relation, sources, relation_ids, destinations, negatives_left[0], negatives_right[0]],
        [half, half, lr_half, lr_half],
        [(CORES * half[0], LANES)],
    )
    rel_got = to_core(rel_send)
    lr_got = to_core(lr_send)

    blocks = []
    for r in range(X_SIZE):
        blocks.append(rel_keep[r * block:(r + 1) * block] + rel_got[r * block:(r + 1) * block])
    mine = scatter(blocks, to_x)
    pieces = []
    for r in range(Y_SIZE):
        pieces.append(mine[r * piece:(r + 1) * piece])
    mine = scatter(pieces, to_y)

    lr_sum = lr_keep + lr_got
    lr_other = to_y(lr_sum, 2)
    packed = (width + 8, rows // CORES)
    new_left, new_right = call(
        adagrad_kernel,
        [where],
        [lr_sum, lr_other, left, right, left_state[None], right_state[None]],
        [packed, packed],
    )
    new_right = to_bucket_before(new_right)
    left_next, left_state_next, right_next, right_state_next = call(
        join_kernel,
        [where],
        [new_left, to_core(new_left), new_right, to_core(new_right)],
        [(width, rows), (1, rows), (width, rows), (1, rows)],
    )

    for bit in (1, 2, 4):
        mine = mine + to_z(mine, bit)
    mine = gather(mine, Y_SIZE, to_y)
    mine = gather(mine, X_SIZE, to_x)
    relation_grad, = call(relation_kernel, [where], [mine, to_core(mine)], [(width, types)], [(CORES * half[0], LANES)])
    return left_next.T, left_state_next[0], right_next.T, right_state_next[0], relation_grad.T


def solution(mesh):
    in_specs = (
        P("dom", None),
        P("dom"),
        P("dom", None),
        P("dom"),
        P(),
        P("dom", "rep"),
        P("dom", "rep"),
        P("dom", "rep"),
        P("dom", "rep", None),
        P("dom", "rep", None),
        P("dom"),
    )
    out_specs = (P("dom", None), P("dom"), P("dom", None), P("dom"), P())
    return jax.shard_map(body, mesh=mesh, in_specs=in_specs, out_specs=out_specs, check_vma=False)
```

```python
import functools

import jax
import jax.numpy as jnp
from jax import lax
from jax.sharding import PartitionSpec as P
from jax.experimental import pallas as pl
from jax.experimental.pallas import tpu as pltpu

MARGIN = 0.1
LEARN_RATE = 0.1
F32 = jnp.float32
BF16 = jnp.bfloat16
NN = (((1,), (0,)), ((), ()))
NT = (((1,), (1,)), ((), ()))


def parts(value):
    high = value.astype(BF16)
    return high, (value - high.astype(F32)).astype(BF16)


def dot(a, b, dims):
    return lax.dot_general(a, b, dims, preferred_element_type=F32)


def dot_picked(value, picks, dims):
    rows = value.shape[0]
    both = dot(jnp.concatenate(parts(value), axis=0), picks, dims)
    return both[:rows] + both[rows:]


def dot_split(a, b, dims):
    rows = a[0].shape[0]
    both = dot(jnp.concatenate(a, axis=0), b[0], dims)
    return both[:rows] + (dot(a[0], b[1], dims) + both[rows:])


def product(v, w):
    return v[0] * w[0] - v[1] * w[1], v[0] * w[1] + v[1] * w[0]


def adjoint(v, w):
    return v[0] * w[0] + v[1] * w[1], v[1] * w[0] - v[0] * w[1]


def halves(x):
    half = x.shape[0] // 2
    return x[:half], x[half:]


def one_hot(ids, rows):
    return (lax.broadcasted_iota(jnp.int32, (rows, ids.shape[1]), 0) == ids).astype(F32)


CORES, X_SIZE, Y_SIZE, Z_SIZE = 2, 4, 4, 8
DEVICES = CORES * X_SIZE * Y_SIZE * Z_SIZE
LANES = 128
VMEM_LIMIT = 32 * 1024 * 1024


def place(dom, rep):
    return rep % 2, dom // 16, (rep // 2) * 2 + (dom // 8) % 2, dom % 8


def here():
    return place(lax.axis_index("dom"), lax.axis_index("rep"))


def device(core, x, y, z):
    return ((x * 2 + y % 2) * 8 + z) * 4 + (y // 2) * 2 + core


def send(value, target):
    pairs = []
    for n in range(DEVICES):
        pairs.append((n, device(*target(*place(n // 4, n % 4)))))
    return lax.ppermute(value, ("dom", "rep"), pairs)


def to_core(value):
    return send(value, lambda core, x, y, z: (1 - core, x, y, z))


def to_first(value, step):
    return send(
        value,
        lambda core, x, y, z: (core, x, (y + step) % Y_SIZE, z) if core else (core, (x + step) % X_SIZE, y, z),
    )


def to_second(value, step):
    return send(
        value,
        lambda core, x, y, z: (core, (x + step) % X_SIZE, y, z) if core else (core, x, (y + step) % Y_SIZE, z),
    )


def to_y(value, step):
    return send(value, lambda core, x, y, z: (core, x, (y + step) % Y_SIZE, z))


def to_z(value, target):
    return send(value, lambda core, x, y, z: (core, x, y, target(z) % Z_SIZE))


def to_bucket_before(value):
    pairs = []
    for n in range(DEVICES):
        pairs.append((n, (n - 4) % DEVICES))
    return lax.ppermute(value, ("dom", "rep"), pairs)


def piece_rows(total):
    block = total // LANES // (CORES * X_SIZE)
    piece = -(-block // (8 * Y_SIZE)) * 8
    return block, piece


def block_spans(width, types, parity):
    block, piece = piece_rows(width * types)
    found = []
    for k, start, size, row in spans(width, types):
        if row // (piece * Y_SIZE) == parity:
            found.append((k, start, size, row))
    return found


def spans(width, types):
    block, piece = piece_rows(width * types)
    pad = piece * Y_SIZE - block
    found = []
    for k in range(types // LANES):
        row, end = k * width, (k + 1) * width
        while row < end:
            stop = min(end, (row // block + 1) * block)
            found.append((k, row - k * width, stop - row, row + (row // block) * pad))
            row = stop
    return found


def piece_at(half, x, y, r, s, piece):
    first, second = jnp.where(half == 0, x, y), jnp.where(half == 0, y, x)
    block = half * X_SIZE + (first + r) % X_SIZE
    return pl.multiple_of((block * Y_SIZE + (second + s) % Y_SIZE) * piece, 8)


def grad_kernel(counts_ref, left_ref, right_ref, rel_ref, src_ref, rid_ref, dst_ref, negl_ref, negr_ref, *refs):
    send_refs, keep_refs = refs[:X_SIZE], refs[X_SIZE:2 * X_SIZE]
    q_ref, p_ref, gr_ref, gl_ref, ds_ref, dt_ref, rows_ref, near_left_ref, near_right_ref, near_rel_ref, sems = refs[2 * X_SIZE:]
    core, x, y, _ = here()
    fetches = []
    for n, pair in enumerate(((left_ref, near_left_ref), (right_ref, near_right_ref), (rel_ref, near_rel_ref))):
        fetches.append(pltpu.make_async_copy(*pair, sems.at[n]))
    for fetch in fetches:
        fetch.start()
    slots = src_ref.shape[1]
    rows = left_ref.shape[1]
    types = rel_ref.shape[1]
    negatives = negl_ref.shape[1]
    count_right = jnp.sum(one_hot(negr_ref[...], rows), axis=1, keepdims=True)
    count_left = jnp.sum(one_hot(negl_ref[...], rows), axis=1, keepdims=True)
    pick_src = one_hot(src_ref[...], rows).astype(BF16)
    pick_dst = one_hot(dst_ref[...], rows).astype(BF16)
    pick_rel = one_hot(rid_ref[...], types).astype(BF16)
    fetches[0].wait()
    left = near_left_ref[...]
    source = dot_picked(left, pick_src, NN)
    left_parts, left_rows = parts(left), parts(left.T)
    fetches[1].wait()
    right = near_right_ref[...]
    target = dot_picked(right, pick_dst, NN)
    right_parts, right_rows = parts(right), parts(right.T)
    fetches[2].wait()
    weight = dot_picked(near_rel_ref[...], pick_rel, NN)
    s, t, w = halves(source), halves(target), halves(weight)
    q = jnp.concatenate(product(s, w), axis=0)
    p = jnp.concatenate(adjoint(t, w), axis=0)
    positive = jnp.sum(q * target, axis=0, keepdims=True)
    q_parts, p_parts = parts(q), parts(p)
    slot = lax.broadcasted_iota(jnp.int32, (1, slots), 1)
    live = (slot + lax.axis_index("rep") * slots < counts_ref[0]).astype(F32) * (1.0 / negatives)
    offset = MARGIN - positive
    g_right = jax.nn.sigmoid(offset + dot_split(right_rows, q_parts, NN)) * count_right * live
    g_left = jax.nn.sigmoid(offset + dot_split(left_rows, p_parts, NN)) * count_left * live
    d_pos = -(jnp.sum(g_right, axis=0, keepdims=True) + jnp.sum(g_left, axis=0, keepdims=True))
    gr_parts, gl_parts = parts(g_right), parts(g_left)
    d_q = dot_split(right_parts, gr_parts, NN) + d_pos * target
    d_p = dot_split(left_parts, gl_parts, NN)
    dq, dp = halves(d_q), halves(d_p)
    a, b = adjoint(dq, s), adjoint(dp, t)
    d_w = jnp.concatenate([a[0] + b[0], a[1] - b[1]], axis=0)
    d_relation = dot_picked(d_w, pick_rel, NT)
    width = d_relation.shape[0]
    block, piece = piece_rows(width * types)
    pad = piece * Y_SIZE - block
    if pad:
        for k in range(CORES * X_SIZE):
            rows_ref[(k + 1) * (block + pad) - pad:(k + 1) * (block + pad), :] = jnp.zeros((pad, LANES), F32)
    for k, start, size, row in spans(width, types):
        rows_ref[row:row + size, :] = d_relation[start:start + size, k * LANES:(k + 1) * LANES]
    for out_refs, half in ((send_refs, 1 - core), (keep_refs, core)):
        for r in range(X_SIZE):
            for s in range(Y_SIZE):
                out_refs[r][s * piece:(s + 1) * piece, :] = rows_ref[pl.ds(piece_at(half, x, y, r, s, piece), piece), :]
    q_ref[...], p_ref[...] = q, p
    gr_ref[...], gl_ref[...] = g_right, g_left
    ds_ref[...] = jnp.concatenate(adjoint(dq, w), axis=0)
    dt_ref[...] = jnp.concatenate(product(dp, w), axis=0) + d_pos * q


def rows_kernel(src_ref, dst_ref, q_ref, p_ref, gr_ref, gl_ref, ds_ref, dt_ref, send_ref, keep_ref):
    width = q_ref.shape[0]
    rows = gr_ref.shape[0]
    half = rows // CORES
    first = here()[0] == 0
    for at, ids_ref, edge_ref, score_ref, picked_ref in (
        (0, src_ref, p_ref, gl_ref, ds_ref),
        (width, dst_ref, q_ref, gr_ref, dt_ref),
    ):
        picks = one_hot(ids_ref[...], rows).astype(BF16)
        grad = dot_split(parts(edge_ref[...]), parts(score_ref[...]), NT) + dot_picked(picked_ref[...], picks, NT)
        low, high = grad[:, :half], grad[:, half:]
        keep_ref[at:at + width, :] = jnp.where(first, low, high)
        send_ref[at:at + width, :] = jnp.where(first, high, low)


WHOLE = pl.BlockSpec(memory_space=pltpu.VMEM)


def near(value):
    return pltpu.with_memory_space_constraint(value, pltpu.VMEM)


def far(value):
    return pltpu.with_memory_space_constraint(value, pltpu.HBM)


def call(kernel, specs, arrays, shapes, scratch=(), own=True):
    return pl.pallas_call(
        kernel,
        out_shape=[pltpu.VMEM(shape, F32) if own else jax.ShapeDtypeStruct(shape, F32) for shape in shapes],
        in_specs=list(specs) + [WHOLE] * (len(arrays) - len(specs)),
        out_specs=[WHOLE] * len(shapes),
        scratch_shapes=list(scratch),
        compiler_params=pltpu.CompilerParams(vmem_limit_bytes=VMEM_LIMIT),
    )(*arrays)


def adagrad_kernel(kept_ref, got_ref, left_ref, right_ref, left_state_ref, right_state_ref, new_left_ref, new_right_ref):
    width = left_ref.shape[0]
    first = here()[0] == 0
    for at, rows_ref, state_ref, out_ref in (
        (0, left_ref, left_state_ref, new_left_ref),
        (width, right_ref, right_state_ref, new_right_ref),
    ):
        half = rows_ref.shape[1] // CORES
        gradient = kept_ref[at:at + width, :] + got_ref[at:at + width, :]
        embedding = jnp.where(first, rows_ref[:, :half], rows_ref[:, half:])
        state = jnp.where(first, state_ref[:, :half], state_ref[:, half:])
        new_state = state + jnp.sum(gradient * gradient, axis=0, keepdims=True) * (1.0 / width)
        out_ref[:width, :] = embedding - gradient * (LEARN_RATE / jnp.sqrt(new_state))
        out_ref[width:, :] = jnp.broadcast_to(new_state, (8, half))


def join_kernel(own_left_ref, other_left_ref, own_right_ref, other_right_ref, left_ref, left_state_ref, right_ref, right_state_ref):
    first = here()[0] == 0
    width = left_ref.shape[0]
    half = own_left_ref.shape[1]
    for own_ref, other_ref, rows_ref, state_ref in (
        (own_left_ref, other_left_ref, left_ref, left_state_ref),
        (own_right_ref, other_right_ref, right_ref, right_state_ref),
    ):
        own, other = own_ref[...], other_ref[...]
        for at, value in ((0, jnp.where(first, own, other)), (half, jnp.where(first, other, own))):
            rows_ref[:, at:at + half] = value[:width]
            state_ref[:, at:at + half] = value[width:width + 1]


def relation_kernel(steps, *refs):
    count = 2 * len(steps)
    in_refs, (out_ref, rows_ref, sems) = refs[-3 - count:-3], refs[-3:]
    core, x, y, _ = here()
    width, types = out_ref.shape
    block, piece = piece_rows(width * types)
    lanes_each = block * LANES // width
    for n, in_ref in enumerate(in_refs):
        half = core if n % 2 == 0 else 1 - core
        second = jnp.where(half == 0, y, x)
        for s in range(Y_SIZE):
            to = pl.multiple_of((second + s) % Y_SIZE * piece, 8)
            rows_ref[n, pl.ds(to, piece), :] = in_ref[s * piece:(s + 1) * piece, :]
    for begin in (True, False):
        for n in range(count):
            half = core if n % 2 == 0 else 1 - core
            first = (jnp.where(half == 0, x, y) + steps[n // 2]) % X_SIZE
            for low in range(2):

                @pl.when(first % 2 == low)
                def _():
                    at = 0
                    for i, (k, start, size, _) in enumerate(block_spans(width, types, low)):
                        lane = (half * X_SIZE + first - low) * lanes_each + k * LANES
                        copy = pltpu.make_async_copy(
                            rows_ref.at[n, pl.ds(at, size), :],
                            out_ref.at[pl.ds(start, size), pl.ds(pl.multiple_of(lane, LANES), LANES)],
                            sems.at[n, i],
                        )
                        if begin:
                            copy.start()
                        else:
                            copy.wait()
                        at += size


def put_relation(steps, blocks, sofar, width, types):
    piece = piece_rows(width * types)[1]
    anywhere = pl.BlockSpec(memory_space=pl.ANY)
    before = [] if sofar is None else [sofar]
    count = len(blocks)
    return pl.pallas_call(
        functools.partial(relation_kernel, steps),
        out_shape=jax.ShapeDtypeStruct((width, types), F32),
        in_specs=[anywhere] * len(before) + [WHOLE] * count,
        out_specs=anywhere,
        scratch_shapes=[pltpu.VMEM((count, piece * Y_SIZE, LANES), F32), pltpu.SemaphoreType.DMA((count, 2))],
        input_output_aliases={0: 0} if before else {},
        compiler_params=pltpu.CompilerParams(vmem_limit_bytes=VMEM_LIMIT),
    )(*before, *[near(value) for value in blocks])


def scatter(pieces, move):
    return sum([move(pieces[r], r) for r in (2, 1, 3)], pieces[0])


def gather(own, count, move):
    got = {r: move(own, (count - r) % count) for r in (2, 3, 1)}
    return [own] + [got[r] for r in range(1, count)]


def after(value, *others):
    return lax.optimization_barrier((value, *others))


def body(left_embedding, left_state, right_embedding, right_state, relation, sources, relation_ids, destinations, negatives_left, negatives_right, edge_counts):
    left, right, relation = left_embedding.T, right_embedding.T, relation.T
    width, types = relation.shape
    rows = left.shape[1]
    edges = sources.shape[1]
    piece = piece_rows(width * types)[1]
    block = (piece * Y_SIZE, LANES)
    scalar = pl.BlockSpec(memory_space=pltpu.SMEM)
    found = call(
        grad_kernel,
        [scalar] + [pl.BlockSpec(memory_space=pl.ANY)] * 3,
        [edge_counts] + [far(value) for value in (left, right, relation, sources, relation_ids, destinations, negatives_left[0], negatives_right[0])],
        [block] * (2 * X_SIZE) + [(width, edges)] * 2 + [(rows, edges)] * 2 + [(width, edges)] * 2,
        [pltpu.VMEM((CORES * X_SIZE * block[0], LANES), F32), pltpu.VMEM(left.shape, F32), pltpu.VMEM(right.shape, F32), pltpu.VMEM(relation.shape, F32), pltpu.SemaphoreType.DMA((3,))],
    )
    rel_send, rel_keep, saved = found[:X_SIZE], found[X_SIZE:2 * X_SIZE], found[2 * X_SIZE:]

    blocks = {}
    for r in (2, 1, 3, 0):
        blocks[r] = rel_keep[r] + to_core(rel_send[r])
    blocks[3], *saved = after(blocks[3], *saved)
    mine = scatter([blocks[r] for r in range(X_SIZE)], to_first)

    lr_half = (2 * width, rows // CORES)
    lr_send, lr_keep = call(rows_kernel, [], [far(sources), far(destinations)] + [near(value) for value in saved], [lr_half, lr_half])
    lr_sum = lr_keep + to_core(lr_send)

    pieces = []
    for r in range(Y_SIZE):
        pieces.append(mine[r * piece:(r + 1) * piece])
    mine = scatter(pieces, to_second)

    mine = mine + to_z(mine, lambda z: z ^ 1)
    mine, lr_sum = after(mine, lr_sum)
    lr_other = to_y(lr_sum, 2)
    opposite = to_z(mine, lambda z: z ^ 5)
    opposite, lr_sum, lr_other = after(opposite, lr_sum, lr_other)
    packed = (width + 8, rows // CORES)
    new_left, new_right = call(
        adagrad_kernel,
        [],
        [near(lr_sum), near(lr_other)] + [far(value) for value in (left, right, left_state[None], right_state[None])],
        [packed, packed],
    )
    new_right = to_bucket_before(new_right)
    other_left = to_core(new_left)
    mine = (mine + opposite) + (to_z(mine, lambda z: z + 2) + to_z(mine, lambda z: z - 2))

    mine = jnp.concatenate(gather(mine, Y_SIZE, to_second), axis=0)
    mine, new_left, other_left, new_right = after(mine, new_left, other_left, new_right)
    own = gather(mine, X_SIZE, to_first)
    own[2], new_right = after(own[2], new_right)
    left_next, left_state_next, right_next, right_state_next = call(
        join_kernel,
        [],
        [near(value) for value in (new_left, other_left, new_right, to_core(new_right))],
        [(width, rows), (1, rows), (width, rows), (1, rows)],
        own=False,
    )
    relation_grad = put_relation((0, 2), [own[0], to_core(own[0]), own[2], to_core(own[2])], None, width, types)
    last = own[1]
    last, relation_grad, left_next, left_state_next, right_next, right_state_next = after(
        last, relation_grad, left_next, left_state_next, right_next, right_state_next
    )
    relation_grad = put_relation((3,), [own[3], to_core(own[3])], relation_grad, width, types)
    relation_grad = put_relation((1,), [last, to_core(last)], relation_grad, width, types)
    return left_next.T, left_state_next[0], right_next.T, right_state_next[0], relation_grad.T


def solution(mesh):
    in_specs = (
        P("dom", None),
        P("dom"),
        P("dom", None),
        P("dom"),
        P(),
        P("dom", "rep"),
        P("dom", "rep"),
        P("dom", "rep"),
        P("dom", "rep", None),
        P("dom", "rep", None),
        P("dom"),
    )
    out_specs = (P("dom", None), P("dom"), P("dom", None), P("dom"), P())
    return jax.shard_map(body, mesh=mesh, in_specs=in_specs, out_specs=out_specs, check_vma=False)
```

```python
import functools

import jax
import jax.numpy as jnp
from jax import lax
from jax.sharding import PartitionSpec as P
from jax.experimental import pallas as pl
from jax.experimental.pallas import tpu as pltpu

MARGIN = 0.1
LEARN_RATE = 0.1
F32 = jnp.float32
BF16 = jnp.bfloat16
NN = (((1,), (0,)), ((), ()))
NT = (((1,), (1,)), ((), ()))


def parts(value):
    high = value.astype(BF16)
    return high, (value - high.astype(F32)).astype(BF16)


def dot(a, b, dims):
    return lax.dot_general(a, b, dims, preferred_element_type=F32)


def dot_picked(value, picks, dims):
    rows = value.shape[0]
    both = dot(jnp.concatenate(parts(value), axis=0), picks, dims)
    return both[:rows] + both[rows:]


def dot_split(a, b, dims):
    rows = a[0].shape[0]
    both = dot(jnp.concatenate(a, axis=0), b[0], dims)
    return both[:rows] + (dot(a[0], b[1], dims) + both[rows:])


def product(v, w):
    return v[0] * w[0] - v[1] * w[1], v[0] * w[1] + v[1] * w[0]


def adjoint(v, w):
    return v[0] * w[0] + v[1] * w[1], v[1] * w[0] - v[0] * w[1]


def halves(x):
    half = x.shape[0] // 2
    return x[:half], x[half:]


def one_hot(ids, rows):
    return (lax.broadcasted_iota(jnp.int32, (rows, ids.shape[1]), 0) == ids).astype(F32)


CORES, X_SIZE, Y_SIZE, Z_SIZE = 2, 4, 4, 8
DEVICES = CORES * X_SIZE * Y_SIZE * Z_SIZE
LANES = 128
VMEM_LIMIT = 32 * 1024 * 1024
COST = 16 * 1024 * 1024


def place(dom, rep):
    return rep % 2, dom // 16, (rep // 2) * 2 + (dom // 8) % 2, dom % 8


def here():
    return place(lax.axis_index("dom"), lax.axis_index("rep"))


def device(core, x, y, z):
    return ((x * 2 + y % 2) * 8 + z) * 4 + (y // 2) * 2 + core


def send(value, target):
    pairs = []
    for n in range(DEVICES):
        pairs.append((n, device(*target(*place(n // 4, n % 4)))))
    return lax.ppermute(value, ("dom", "rep"), pairs)


def to_core(value):
    return send(value, lambda core, x, y, z: (1 - core, x, y, z))


def to_first(value, step):
    return send(
        value,
        lambda core, x, y, z: (core, x, (y + step) % Y_SIZE, z) if core else (core, (x + step) % X_SIZE, y, z),
    )


def to_second(value, step):
    return send(
        value,
        lambda core, x, y, z: (core, (x + step) % X_SIZE, y, z) if core else (core, x, (y + step) % Y_SIZE, z),
    )


def to_y(value, step):
    return send(value, lambda core, x, y, z: (core, x, (y + step) % Y_SIZE, z))


def to_z(value, target):
    return send(value, lambda core, x, y, z: (core, x, y, target(z) % Z_SIZE))


def to_bucket_before(value):
    pairs = []
    for n in range(DEVICES):
        pairs.append((n, (n - 4) % DEVICES))
    return lax.ppermute(value, ("dom", "rep"), pairs)


def piece_rows(total):
    block = total // LANES // (CORES * X_SIZE)
    piece = -(-block // (8 * Y_SIZE)) * 8
    return block, piece


def block_spans(width, types, parity):
    block, piece = piece_rows(width * types)
    found = []
    for k, start, size, row in spans(width, types):
        if row // (piece * Y_SIZE) == parity:
            found.append((k, start, size, row))
    return found


def spans(width, types):
    block, piece = piece_rows(width * types)
    pad = piece * Y_SIZE - block
    found = []
    for k in range(types // LANES):
        row, end = k * width, (k + 1) * width
        while row < end:
            stop = min(end, (row // block + 1) * block)
            found.append((k, row - k * width, stop - row, row + (row // block) * pad))
            row = stop
    return found


def piece_at(half, x, y, r, s, piece):
    first, second = jnp.where(half == 0, x, y), jnp.where(half == 0, y, x)
    return pl.multiple_of(((first + r) % X_SIZE * Y_SIZE + (second + s) % Y_SIZE) * piece, 8)


def grad_kernel(counts_ref, left_ref, right_ref, rel_ref, src_ref, rid_ref, dst_ref, negl_ref, negr_ref, *refs):
    dw_ref, pick_ref, q_ref, p_ref, gr_ref, gl_ref, ds_ref, dt_ref, near_left_ref, near_right_ref, near_rel_ref, sems = refs
    fetches = []
    for n, pair in enumerate(((left_ref, near_left_ref), (right_ref, near_right_ref), (rel_ref, near_rel_ref))):
        fetches.append(pltpu.make_async_copy(*pair, sems.at[n]))
    for fetch in fetches:
        fetch.start()
    slots = src_ref.shape[1]
    rows = left_ref.shape[1]
    types = rel_ref.shape[1]
    negatives = negl_ref.shape[1]
    count_right = jnp.sum(one_hot(negr_ref[...], rows), axis=1, keepdims=True)
    count_left = jnp.sum(one_hot(negl_ref[...], rows), axis=1, keepdims=True)
    pick_src = one_hot(src_ref[...], rows).astype(BF16)
    pick_dst = one_hot(dst_ref[...], rows).astype(BF16)
    pick_rel = one_hot(rid_ref[...], types).astype(BF16)
    fetches[0].wait()
    left = near_left_ref[...]
    source = dot_picked(left, pick_src, NN)
    left_parts, left_rows = parts(left), parts(left.T)
    fetches[1].wait()
    right = near_right_ref[...]
    target = dot_picked(right, pick_dst, NN)
    right_parts, right_rows = parts(right), parts(right.T)
    fetches[2].wait()
    weight = dot_picked(near_rel_ref[...], pick_rel, NN)
    s, t, w = halves(source), halves(target), halves(weight)
    q = jnp.concatenate(product(s, w), axis=0)
    p = jnp.concatenate(adjoint(t, w), axis=0)
    positive = jnp.sum(q * target, axis=0, keepdims=True)
    q_parts, p_parts = parts(q), parts(p)
    slot = lax.broadcasted_iota(jnp.int32, (1, slots), 1)
    live = (slot + lax.axis_index("rep") * slots < counts_ref[0]).astype(F32) * (1.0 / negatives)
    offset = MARGIN - positive
    g_right = jax.nn.sigmoid(offset + dot_split(right_rows, q_parts, NN)) * count_right * live
    g_left = jax.nn.sigmoid(offset + dot_split(left_rows, p_parts, NN)) * count_left * live
    d_pos = -(jnp.sum(g_right, axis=0, keepdims=True) + jnp.sum(g_left, axis=0, keepdims=True))
    gr_parts, gl_parts = parts(g_right), parts(g_left)
    d_q = dot_split(right_parts, gr_parts, NN) + d_pos * target
    d_p = dot_split(left_parts, gl_parts, NN)
    dq, dp = halves(d_q), halves(d_p)
    a, b = adjoint(dq, s), adjoint(dp, t)
    d_w = jnp.concatenate([a[0] + b[0], a[1] - b[1]], axis=0)
    dw_ref[...], pick_ref[...] = d_w, pick_rel
    q_ref[...], p_ref[...] = q, p
    gr_ref[...], gl_ref[...] = g_right, g_left
    ds_ref[...] = jnp.concatenate(adjoint(dq, w), axis=0)
    dt_ref[...] = jnp.concatenate(product(dp, w), axis=0) + d_pos * q


def blocks_kernel(mine, dw_ref, pick_ref, *refs):
    out_refs, rows_ref = refs[:-1], refs[-1]
    core, x, y, _ = here()
    half = core if mine else 1 - core
    width, types = dw_ref.shape[0], pick_ref.shape[0] // CORES
    block, piece = piece_rows(width * types * CORES)
    pad = piece * Y_SIZE - block
    picks = pick_ref[pl.ds(pl.multiple_of(half * types, LANES), types), :]
    grad = dot_picked(dw_ref[...], picks, NT)
    if pad:
        for k in range(X_SIZE):
            rows_ref[(k + 1) * (block + pad) - pad:(k + 1) * (block + pad), :] = jnp.zeros((pad, LANES), F32)
    for k, start, size, row in spans(width, types * CORES):
        if k < types // LANES:
            rows_ref[row:row + size, :] = grad[start:start + size, k * LANES:(k + 1) * LANES]
    for r, out_ref in enumerate(out_refs):
        for s in range(Y_SIZE):
            at = piece_at(half, x, y, r, s, piece)
            out_ref[s * piece:(s + 1) * piece, :] = rows_ref[pl.ds(at, piece), :]


def rows_kernel(src_ref, dst_ref, q_ref, p_ref, gr_ref, gl_ref, ds_ref, dt_ref, send_ref, keep_ref):
    width = q_ref.shape[0]
    rows = gr_ref.shape[0]
    half = rows // CORES
    first = here()[0] == 0
    for at, ids_ref, edge_ref, score_ref, picked_ref in (
        (0, src_ref, p_ref, gl_ref, ds_ref),
        (width, dst_ref, q_ref, gr_ref, dt_ref),
    ):
        picks = one_hot(ids_ref[...], rows).astype(BF16)
        grad = dot_split(parts(edge_ref[...]), parts(score_ref[...]), NT) + dot_picked(picked_ref[...], picks, NT)
        low, high = grad[:, :half], grad[:, half:]
        keep_ref[at:at + width, :] = jnp.where(first, low, high)
        send_ref[at:at + width, :] = jnp.where(first, high, low)


WHOLE = pl.BlockSpec(memory_space=pltpu.VMEM)


def near(value):
    return pltpu.with_memory_space_constraint(value, pltpu.VMEM)


def far(value):
    return pltpu.with_memory_space_constraint(value, pltpu.HBM)


def call(kernel, specs, arrays, shapes, scratch=()):
    return pl.pallas_call(
        kernel,
        out_shape=[pltpu.VMEM(shape[0], shape[1]) if isinstance(shape[0], tuple) else pltpu.VMEM(shape, F32) for shape in shapes],
        in_specs=list(specs) + [WHOLE] * (len(arrays) - len(specs)),
        out_specs=[WHOLE] * len(shapes),
        scratch_shapes=list(scratch),
        compiler_params=pltpu.CompilerParams(vmem_limit_bytes=VMEM_LIMIT),
        cost_estimate=pl.CostEstimate(flops=0, transcendentals=0, bytes_accessed=COST),
    )(*arrays)


def adagrad_kernel(kept_ref, got_ref, left_ref, right_ref, left_state_ref, right_state_ref, new_left_ref, new_right_ref):
    width = left_ref.shape[0]
    first = here()[0] == 0
    for at, rows_ref, state_ref, out_ref in (
        (0, left_ref, left_state_ref, new_left_ref),
        (width, right_ref, right_state_ref, new_right_ref),
    ):
        half = rows_ref.shape[1] // CORES
        gradient = kept_ref[at:at + width, :] + got_ref[at:at + width, :]
        embedding = jnp.where(first, rows_ref[:, :half], rows_ref[:, half:])
        state = jnp.where(first, state_ref[:, :half], state_ref[:, half:])
        new_state = state + jnp.sum(gradient * gradient, axis=0, keepdims=True) * (1.0 / width)
        out_ref[:width, :] = embedding - gradient * (LEARN_RATE / jnp.sqrt(new_state))
        out_ref[width:, :] = jnp.broadcast_to(new_state, (8, half))


def place_kernel(mine, *refs):
    in_refs, (out_ref, new_rows_ref, new_state_ref) = refs[-X_SIZE - 9:-7], refs[-7:-4]
    rows_ref, joined_ref, state_ref, sems = refs[-4:]
    blocks, (own_ref, other_ref) = in_refs[:X_SIZE], in_refs[X_SIZE:]
    core, x, y, _ = here()
    half = core if mine else 1 - core
    width, types = out_ref.shape
    block, piece = piece_rows(width * types)
    lanes_each = block * LANES // width
    mine_first, mine_second = jnp.where(half == 0, x, y), jnp.where(half == 0, y, x)
    columns = own_ref.shape[1]
    own, other = own_ref[...], other_ref[...]
    for at, value in ((0, jnp.where(core == 0, own, other)), (columns, jnp.where(core == 0, other, own))):
        joined_ref[:, at:at + columns] = value[:width]
        state_ref[:, at:at + columns] = value[width:width + 1]
    copies = [
        pltpu.make_async_copy(joined_ref, new_rows_ref, sems.at[X_SIZE, 0]),
        pltpu.make_async_copy(state_ref, new_state_ref, sems.at[X_SIZE, 1]),
    ]
    for copy in copies:
        copy.start()

    def move(n, begin):
        first = (mine_first + n) % X_SIZE
        for low in range(2):

            @pl.when(first % 2 == low)
            def _():
                at = 0
                for i, (k, start, size, _) in enumerate(block_spans(width, types, low)):
                    lane = (half * X_SIZE + first - low) * lanes_each + k * LANES
                    copy = pltpu.make_async_copy(
                        rows_ref.at[n, pl.ds(at, size), :],
                        out_ref.at[pl.ds(start, size), pl.ds(pl.multiple_of(lane, LANES), LANES)],
                        sems.at[n, i],
                    )
                    if begin:
                        copy.start()
                    else:
                        copy.wait()
                    at += size

    for n, in_ref in enumerate(blocks):
        for s in range(Y_SIZE):
            to = pl.multiple_of((mine_second + s) % Y_SIZE * piece, 8)
            rows_ref[n, pl.ds(to, piece), :] = in_ref[s * piece:(s + 1) * piece, :]
        move(n, True)
    for n in range(X_SIZE):
        move(n, False)
    for copy in copies:
        copy.wait()


def put(mine, blocks, sofar, rows, shapes):
    width, types = shapes[0]
    piece = piece_rows(width * types)[1]
    anywhere = pl.BlockSpec(memory_space=pl.ANY)
    before = [] if sofar is None else [sofar]
    return pl.pallas_call(
        functools.partial(place_kernel, mine),
        out_shape=[jax.ShapeDtypeStruct(shape, F32) for shape in shapes],
        in_specs=[anywhere] * len(before) + [WHOLE] * (X_SIZE + 2),
        out_specs=[anywhere] * 3,
        scratch_shapes=[
            pltpu.VMEM((X_SIZE, piece * Y_SIZE, LANES), F32),
            pltpu.VMEM(shapes[1], F32),
            pltpu.VMEM(shapes[2], F32),
            pltpu.SemaphoreType.DMA((X_SIZE + 1, 2)),
        ],
        input_output_aliases={0: 0} if before else {},
        compiler_params=pltpu.CompilerParams(vmem_limit_bytes=VMEM_LIMIT),
        cost_estimate=pl.CostEstimate(flops=0, transcendentals=0, bytes_accessed=COST),
    )(*before, *[near(value) for value in list(blocks) + list(rows)])


def scatter(pieces, move):
    return sum([move(pieces[r], r) for r in (2, 1, 3)], pieces[0])


def gather(own, count, move):
    got = {r: move(own, (count - r) % count) for r in (2, 3, 1)}
    return [own] + [got[r] for r in range(1, count)]


def after(value, *others):
    return lax.optimization_barrier((value, *others))


def body(left_embedding, left_state, right_embedding, right_state, relation, sources, relation_ids, destinations, negatives_left, negatives_right, edge_counts):
    left, right, relation = left_embedding.T, right_embedding.T, relation.T
    width, types = relation.shape
    rows = left.shape[1]
    edges = sources.shape[1]
    piece = piece_rows(width * types)[1]
    block = (piece * Y_SIZE, LANES)
    scalar = pl.BlockSpec(memory_space=pltpu.SMEM)
    found = call(
        grad_kernel,
        [scalar] + [pl.BlockSpec(memory_space=pl.ANY)] * 3,
        [edge_counts] + [far(value) for value in (left, right, relation, sources, relation_ids, destinations, negatives_left[0], negatives_right[0])],
        [(width, edges), ((types, edges), BF16)] + [(width, edges)] * 2 + [(rows, edges)] * 2 + [(width, edges)] * 2,
        [pltpu.VMEM(left.shape, F32), pltpu.VMEM(right.shape, F32), pltpu.VMEM(relation.shape, F32), pltpu.SemaphoreType.DMA((3,))],
    )
    by_relation, saved = [near(value) for value in found[:2]], found[2:]
    staging = [pltpu.VMEM((X_SIZE * block[0], LANES), F32)]
    rel_send = call(functools.partial(blocks_kernel, False), [], by_relation, [block] * X_SIZE, staging)
    rel_keep = call(functools.partial(blocks_kernel, True), [], by_relation, [block] * X_SIZE, staging)

    blocks = {}
    for r in (2, 1, 3, 0):
        blocks[r] = rel_keep[r] + to_core(rel_send[r])
    blocks[3], *saved = after(blocks[3], *saved)
    mine = scatter([blocks[r] for r in range(X_SIZE)], to_first)

    lr_half = (2 * width, rows // CORES)
    lr_send, lr_keep = call(rows_kernel, [], [far(sources), far(destinations)] + [near(value) for value in saved], [lr_half, lr_half])
    lr_sum = lr_keep + to_core(lr_send)

    pieces = []
    for r in range(Y_SIZE):
        pieces.append(mine[r * piece:(r + 1) * piece])
    mine = scatter(pieces, to_second)

    mine = mine + to_z(mine, lambda z: z ^ 1)
    mine, lr_sum = after(mine, lr_sum)
    lr_other = to_y(lr_sum, 2)
    opposite = to_z(mine, lambda z: z ^ 5)
    mine = (mine + opposite) + (to_z(mine, lambda z: z + 2) + to_z(mine, lambda z: z - 2))
    found = gather(mine, Y_SIZE, to_second)
    found[2], lr_sum, lr_other = after(found[2], lr_sum, lr_other)
    packed = (width + 8, rows // CORES)
    new_left, new_right = call(
        adagrad_kernel,
        [],
        [near(lr_sum), near(lr_other)] + [far(value) for value in (left, right, left_state[None], right_state[None])],
        [packed, packed],
    )
    *found, new_left, new_right = after(*found, new_left, new_right)
    new_right = to_bucket_before(new_right)
    other_left = to_core(new_left)
    *found, other_left = after(*found, other_left)
    own = gather(jnp.concatenate(found, axis=0), X_SIZE, to_first)
    other_right = to_core(new_right)
    other = [to_core(value) for value in own]
    shapes = [(width, types), (width, rows), (1, rows)]
    relation_grad, left_next, left_state_next = put(True, own, None, [new_left, other_left], shapes)
    relation_grad, right_next, right_state_next = put(False, other, relation_grad, [new_right, other_right], shapes)
    return left_next.T, left_state_next[0], right_next.T, right_state_next[0], relation_grad.T


def solution(mesh):
    in_specs = (
        P("dom", None),
        P("dom"),
        P("dom", None),
        P("dom"),
        P(),
        P("dom", "rep"),
        P("dom", "rep"),
        P("dom", "rep"),
        P("dom", "rep", None),
        P("dom", "rep", None),
        P("dom"),
    )
    out_specs = (P("dom", None), P("dom"), P("dom", None), P("dom"), P())
    return jax.shard_map(body, mesh=mesh, in_specs=in_specs, out_specs=out_specs, check_vma=False)
```

```python
import functools

import jax
import jax.numpy as jnp
from jax import lax
from jax.sharding import PartitionSpec as P
from jax.experimental import pallas as pl
from jax.experimental.pallas import tpu as pltpu

MARGIN = 0.1
LEARN_RATE = 0.1
F32 = jnp.float32
BF16 = jnp.bfloat16
NN = (((1,), (0,)), ((), ()))
NT = (((1,), (1,)), ((), ()))


def parts(value):
    high = value.astype(BF16)
    return high, (value - high.astype(F32)).astype(BF16)


def dot(a, b, dims):
    return lax.dot_general(a, b, dims, preferred_element_type=F32)


def dot_picked(value, picks, dims):
    rows = value.shape[0]
    both = dot(jnp.concatenate(parts(value), axis=0), picks, dims)
    return both[:rows] + both[rows:]


def dot_split(a, b, dims):
    rows = a[0].shape[0]
    both = dot(jnp.concatenate(a, axis=0), b[0], dims)
    return both[:rows] + (dot(a[0], b[1], dims) + both[rows:])


def product(v, w):
    return v[0] * w[0] - v[1] * w[1], v[0] * w[1] + v[1] * w[0]


def adjoint(v, w):
    return v[0] * w[0] + v[1] * w[1], v[1] * w[0] - v[0] * w[1]


def halves(x):
    half = x.shape[0] // 2
    return x[:half], x[half:]


def one_hot(ids, rows):
    return (lax.broadcasted_iota(jnp.int32, (rows, ids.shape[1]), 0) == ids).astype(F32)


CORES, X_SIZE, Y_SIZE, Z_SIZE = 2, 4, 4, 8
DEVICES = CORES * X_SIZE * Y_SIZE * Z_SIZE
LANES = 128
VMEM_LIMIT = 32 * 1024 * 1024
COST = 16 * 1024 * 1024


def place(dom, rep):
    return rep % 2, dom // 16, (rep // 2) * 2 + (dom // 8) % 2, dom % 8


def here():
    return place(lax.axis_index("dom"), lax.axis_index("rep"))


def device(core, x, y, z):
    return ((x * 2 + y % 2) * 8 + z) * 4 + (y // 2) * 2 + core


def send(value, target):
    pairs = []
    for n in range(DEVICES):
        pairs.append((n, device(*target(*place(n // 4, n % 4)))))
    return lax.ppermute(value, ("dom", "rep"), pairs)


def to_core(value):
    return send(value, lambda core, x, y, z: (1 - core, x, y, z))


def to_first(value, step):
    return send(
        value,
        lambda core, x, y, z: (core, x, (y + step) % Y_SIZE, z) if core else (core, (x + step) % X_SIZE, y, z),
    )


def to_second(value, step):
    return send(
        value,
        lambda core, x, y, z: (core, (x + step) % X_SIZE, y, z) if core else (core, x, (y + step) % Y_SIZE, z),
    )


def to_y(value, step):
    return send(value, lambda core, x, y, z: (core, x, (y + step) % Y_SIZE, z))


def to_z(value, target):
    return send(value, lambda core, x, y, z: (core, x, y, target(z) % Z_SIZE))


def to_bucket_before(value):
    pairs = []
    for n in range(DEVICES):
        pairs.append((n, (n - 4) % DEVICES))
    return lax.ppermute(value, ("dom", "rep"), pairs)


def piece_rows(total):
    block = total // LANES // (CORES * X_SIZE)
    piece = -(-block // (8 * Y_SIZE)) * 8
    return block, piece


def block_spans(width, types, parity):
    block, piece = piece_rows(width * types)
    found = []
    for k, start, size, row in spans(width, types):
        if row // (piece * Y_SIZE) == parity:
            found.append((k, start, size, row))
    return found


def spans(width, types):
    block, piece = piece_rows(width * types)
    pad = piece * Y_SIZE - block
    found = []
    for k in range(types // LANES):
        row, end = k * width, (k + 1) * width
        while row < end:
            stop = min(end, (row // block + 1) * block)
            found.append((k, row - k * width, stop - row, row + (row // block) * pad))
            row = stop
    return found


def piece_at(half, x, y, r, s, piece):
    first, second = jnp.where(half == 0, x, y), jnp.where(half == 0, y, x)
    return pl.multiple_of(((first + r) % X_SIZE * Y_SIZE + (second + s) % Y_SIZE) * piece, 8)


def grad_kernel(counts_ref, *refs):
    far_refs, near_refs, sems = refs[:8], refs[-9:-1], refs[-1]
    dw_ref, pick_ref, q_ref, p_ref, gr_ref, gl_ref, ds_ref, dt_ref = refs[8:-9]
    fetches = []
    for n, (far_ref, near_ref) in enumerate(zip(far_refs, near_refs)):
        fetches.append(pltpu.make_async_copy(far_ref, near_ref, sems.at[n]))
    for fetch in fetches:
        fetch.start()
    src_ref, rid_ref, dst_ref, negl_ref, negr_ref, near_left_ref, near_right_ref, near_rel_ref = near_refs
    left_ref, right_ref, rel_ref = near_left_ref, near_right_ref, near_rel_ref
    slots = src_ref.shape[1]
    rows = left_ref.shape[1]
    types = rel_ref.shape[1]
    negatives = negl_ref.shape[1]
    for fetch in fetches[:5]:
        fetch.wait()
    count_right = jnp.sum(one_hot(negr_ref[...], rows), axis=1, keepdims=True)
    count_left = jnp.sum(one_hot(negl_ref[...], rows), axis=1, keepdims=True)
    pick_src = one_hot(src_ref[...], rows).astype(BF16)
    pick_dst = one_hot(dst_ref[...], rows).astype(BF16)
    pick_rel = one_hot(rid_ref[...], types).astype(BF16)
    fetches[5].wait()
    left = near_left_ref[...]
    source = dot_picked(left, pick_src, NN)
    left_parts, left_rows = parts(left), parts(left.T)
    fetches[6].wait()
    right = near_right_ref[...]
    target = dot_picked(right, pick_dst, NN)
    right_parts, right_rows = parts(right), parts(right.T)
    fetches[7].wait()
    weight = dot_picked(near_rel_ref[...], pick_rel, NN)
    s, t, w = halves(source), halves(target), halves(weight)
    q = jnp.concatenate(product(s, w), axis=0)
    p = jnp.concatenate(adjoint(t, w), axis=0)
    positive = jnp.sum(q * target, axis=0, keepdims=True)
    q_parts, p_parts = parts(q), parts(p)
    slot = lax.broadcasted_iota(jnp.int32, (1, slots), 1)
    live = (slot + lax.axis_index("rep") * slots < counts_ref[0]).astype(F32) * (1.0 / negatives)
    offset = MARGIN - positive
    g_right = jax.nn.sigmoid(offset + dot_split(right_rows, q_parts, NN)) * count_right * live
    g_left = jax.nn.sigmoid(offset + dot_split(left_rows, p_parts, NN)) * count_left * live
    d_pos = -(jnp.sum(g_right, axis=0, keepdims=True) + jnp.sum(g_left, axis=0, keepdims=True))
    gr_parts, gl_parts = parts(g_right), parts(g_left)
    d_q = dot_split(right_parts, gr_parts, NN) + d_pos * target
    d_p = dot_split(left_parts, gl_parts, NN)
    dq, dp = halves(d_q), halves(d_p)
    a, b = adjoint(dq, s), adjoint(dp, t)
    d_w = jnp.concatenate([a[0] + b[0], a[1] - b[1]], axis=0)
    dw_ref[...], pick_ref[...] = d_w, pick_rel
    q_ref[...], p_ref[...] = q, p
    gr_ref[...], gl_ref[...] = g_right, g_left
    ds_ref[...] = jnp.concatenate(adjoint(dq, w), axis=0)
    dt_ref[...] = jnp.concatenate(product(dp, w), axis=0) + d_pos * q


def blocks_kernel(mine, dw_ref, pick_ref, *refs):
    out_refs, rows_ref = refs[:-1], refs[-1]
    core, x, y, _ = here()
    half = core if mine else 1 - core
    width, types = dw_ref.shape[0], pick_ref.shape[0] // CORES
    block, piece = piece_rows(width * types * CORES)
    pad = piece * Y_SIZE - block
    picks = pick_ref[pl.ds(pl.multiple_of(half * types, LANES), types), :]
    grad = dot_picked(dw_ref[...], picks, NT)
    if pad:
        for k in range(X_SIZE):
            rows_ref[(k + 1) * (block + pad) - pad:(k + 1) * (block + pad), :] = jnp.zeros((pad, LANES), F32)
    for k, start, size, row in spans(width, types * CORES):
        if k < types // LANES:
            rows_ref[row:row + size, :] = grad[start:start + size, k * LANES:(k + 1) * LANES]
    for r, out_ref in enumerate(out_refs):
        for s in range(Y_SIZE):
            at = piece_at(half, x, y, r, s, piece)
            out_ref[s * piece:(s + 1) * piece, :] = rows_ref[pl.ds(at, piece), :]


def rows_kernel(src_ref, dst_ref, q_ref, p_ref, gr_ref, gl_ref, ds_ref, dt_ref, send_ref, keep_ref):
    width = q_ref.shape[0]
    rows = gr_ref.shape[0]
    half = rows // CORES
    first = here()[0] == 0
    for at, ids_ref, edge_ref, score_ref, picked_ref in (
        (0, src_ref, p_ref, gl_ref, ds_ref),
        (width, dst_ref, q_ref, gr_ref, dt_ref),
    ):
        picks = one_hot(ids_ref[...], rows).astype(BF16)
        grad = dot_split(parts(edge_ref[...]), parts(score_ref[...]), NT) + dot_picked(picked_ref[...], picks, NT)
        low, high = grad[:, :half], grad[:, half:]
        keep_ref[at:at + width, :] = jnp.where(first, low, high)
        send_ref[at:at + width, :] = jnp.where(first, high, low)


WHOLE = pl.BlockSpec(memory_space=pltpu.VMEM)


def near(value):
    return pltpu.with_memory_space_constraint(value, pltpu.VMEM)


def far(value):
    return pltpu.with_memory_space_constraint(value, pltpu.HBM)


def call(kernel, specs, arrays, shapes, scratch=(), cost=COST):
    return pl.pallas_call(
        kernel,
        out_shape=[pltpu.VMEM(shape[0], shape[1]) if isinstance(shape[0], tuple) else pltpu.VMEM(shape, F32) for shape in shapes],
        in_specs=list(specs) + [WHOLE] * (len(arrays) - len(specs)),
        out_specs=[WHOLE] * len(shapes),
        scratch_shapes=list(scratch),
        compiler_params=pltpu.CompilerParams(vmem_limit_bytes=VMEM_LIMIT),
        cost_estimate=pl.CostEstimate(flops=0, transcendentals=0, bytes_accessed=cost),
    )(*arrays)


def adagrad_kernel(kept_ref, got_ref, left_ref, right_ref, left_state_ref, right_state_ref, new_left_ref, new_right_ref):
    width = left_ref.shape[0]
    first = here()[0] == 0
    for at, rows_ref, state_ref, out_ref in (
        (0, left_ref, left_state_ref, new_left_ref),
        (width, right_ref, right_state_ref, new_right_ref),
    ):
        half = rows_ref.shape[1] // CORES
        gradient = kept_ref[at:at + width, :] + got_ref[at:at + width, :]
        embedding = jnp.where(first, rows_ref[:, :half], rows_ref[:, half:])
        state = jnp.where(first, state_ref[:, :half], state_ref[:, half:])
        new_state = state + jnp.sum(gradient * gradient, axis=0, keepdims=True) * (1.0 / width)
        out_ref[:width, :] = embedding - gradient * (LEARN_RATE / jnp.sqrt(new_state))
        out_ref[width:, :] = jnp.broadcast_to(new_state, (8, half))


def place_kernel(mine, *refs):
    in_refs, (out_ref, new_rows_ref, new_state_ref) = refs[-X_SIZE - 9:-7], refs[-7:-4]
    rows_ref, joined_ref, state_ref, sems = refs[-4:]
    blocks, (own_ref, other_ref) = in_refs[:X_SIZE], in_refs[X_SIZE:]
    core, x, y, _ = here()
    half = core if mine else 1 - core
    width, types = out_ref.shape
    block, piece = piece_rows(width * types)
    lanes_each = block * LANES // width
    mine_first, mine_second = jnp.where(half == 0, x, y), jnp.where(half == 0, y, x)
    columns = own_ref.shape[1]
    own, other = own_ref[...], other_ref[...]
    for at, value in ((0, jnp.where(core == 0, own, other)), (columns, jnp.where(core == 0, other, own))):
        joined_ref[:, at:at + columns] = value[:width]
        state_ref[:, at:at + columns] = value[width:width + 1]
    copies = [
        pltpu.make_async_copy(joined_ref, new_rows_ref, sems.at[X_SIZE, 0]),
        pltpu.make_async_copy(state_ref, new_state_ref, sems.at[X_SIZE, 1]),
    ]
    for copy in copies:
        copy.start()

    def move(n, begin):
        first = (mine_first + n) % X_SIZE
        for low in range(2):

            @pl.when(first % 2 == low)
            def _():
                at = 0
                for i, (k, start, size, _) in enumerate(block_spans(width, types, low)):
                    lane = (half * X_SIZE + first - low) * lanes_each + k * LANES
                    copy = pltpu.make_async_copy(
                        rows_ref.at[n, pl.ds(at, size), :],
                        out_ref.at[pl.ds(start, size), pl.ds(pl.multiple_of(lane, LANES), LANES)],
                        sems.at[n, i],
                    )
                    if begin:
                        copy.start()
                    else:
                        copy.wait()
                    at += size

    for n, in_ref in enumerate(blocks):
        for s in range(Y_SIZE):
            to = pl.multiple_of((mine_second + s) % Y_SIZE * piece, 8)
            rows_ref[n, pl.ds(to, piece), :] = in_ref[s * piece:(s + 1) * piece, :]
        move(n, True)
    for n in range(X_SIZE):
        move(n, False)
    for copy in copies:
        copy.wait()


def put(mine, blocks, sofar, rows, shapes):
    width, types = shapes[0]
    piece = piece_rows(width * types)[1]
    anywhere = pl.BlockSpec(memory_space=pl.ANY)
    before = [] if sofar is None else [sofar]
    return pl.pallas_call(
        functools.partial(place_kernel, mine),
        out_shape=[jax.ShapeDtypeStruct(shape, F32) for shape in shapes],
        in_specs=[anywhere] * len(before) + [WHOLE] * (X_SIZE + 2),
        out_specs=[anywhere] * 3,
        scratch_shapes=[
            pltpu.VMEM((X_SIZE, piece * Y_SIZE, LANES), F32),
            pltpu.VMEM(shapes[1], F32),
            pltpu.VMEM(shapes[2], F32),
            pltpu.SemaphoreType.DMA((X_SIZE + 1, 2)),
        ],
        input_output_aliases={0: 0} if before else {},
        compiler_params=pltpu.CompilerParams(vmem_limit_bytes=VMEM_LIMIT),
        cost_estimate=pl.CostEstimate(flops=0, transcendentals=0, bytes_accessed=COST),
    )(*before, *[near(value) for value in list(blocks) + list(rows)])


def scatter(pieces, move):
    return sum([move(pieces[r], r) for r in (2, 1, 3)], pieces[0])


def gather(own, count, move):
    got = {r: move(own, (count - r) % count) for r in (2, 3, 1)}
    return [own] + [got[r] for r in range(1, count)]


def after(value, *others):
    return lax.optimization_barrier((value, *others))


def body(left_embedding, left_state, right_embedding, right_state, relation, sources, relation_ids, destinations, negatives_left, negatives_right, edge_counts):
    left, right, relation = left_embedding.T, right_embedding.T, relation.T
    width, types = relation.shape
    rows = left.shape[1]
    edges = sources.shape[1]
    piece = piece_rows(width * types)[1]
    block = (piece * Y_SIZE, LANES)
    scalar = pl.BlockSpec(memory_space=pltpu.SMEM)
    given = (sources, relation_ids, destinations, negatives_left[0], negatives_right[0], left, right, relation)
    found = call(
        grad_kernel,
        [scalar] + [pl.BlockSpec(memory_space=pl.ANY)] * len(given),
        [edge_counts] + [far(value) for value in given],
        [(width, edges), ((types, edges), BF16)] + [(width, edges)] * 2 + [(rows, edges)] * 2 + [(width, edges)] * 2,
        [pltpu.VMEM(value.shape, value.dtype) for value in given] + [pltpu.SemaphoreType.DMA((len(given),))],
    )
    by_relation, saved = [near(value) for value in found[:2]], found[2:]
    staging = [pltpu.VMEM((X_SIZE * block[0], LANES), F32)]
    rel_send = call(functools.partial(blocks_kernel, False), [], by_relation, [block] * X_SIZE, staging)
    rel_keep = call(functools.partial(blocks_kernel, True), [], by_relation, [block] * X_SIZE, staging)

    blocks = {}
    for r in (2, 1, 3, 0):
        blocks[r] = rel_keep[r] + to_core(rel_send[r])
    blocks[3], *saved = after(blocks[3], *saved)
    mine = scatter([blocks[r] for r in range(X_SIZE)], to_first)

    lr_half = (2 * width, rows // CORES)
    lr_send, lr_keep = call(rows_kernel, [], [far(sources), far(destinations)] + [near(value) for value in saved], [lr_half, lr_half])
    lr_sum = lr_keep + to_core(lr_send)

    pieces = []
    for r in range(Y_SIZE):
        pieces.append(mine[r * piece:(r + 1) * piece])
    mine = scatter(pieces, to_second)

    mine = mine + to_z(mine, lambda z: z ^ 1)
    mine, lr_sum = after(mine, lr_sum)
    lr_other = to_y(lr_sum, 2)
    opposite = to_z(mine, lambda z: z ^ 5)
    nearer = to_z(mine, lambda z: z + 1 if z % 2 else z - 1)
    other_side = to_z(mine, lambda z: z + 2 if z % 2 else z - 2)
    mine = (mine + opposite) + (nearer + other_side)
    found = gather(mine, Y_SIZE, to_second)
    found[2], lr_sum, lr_other = after(found[2], lr_sum, lr_other)
    packed = (width + 8, rows // CORES)
    new_left, new_right = call(
        adagrad_kernel,
        [],
        [near(lr_sum), near(lr_other)] + [far(value) for value in (left, right, left_state[None], right_state[None])],
        [packed, packed],
        cost=0,
    )
    *found, new_left, new_right = after(*found, new_left, new_right)
    new_right = to_bucket_before(new_right)
    other_left = to_core(new_left)
    *found, other_left = after(*found, other_left)
    own = gather(jnp.concatenate(found, axis=0), X_SIZE, to_first)
    other_right = to_core(new_right)
    other = [to_core(value) for value in own]
    shapes = [(width, types), (width, rows), (1, rows)]
    relation_grad, left_next, left_state_next = put(True, own, None, [new_left, other_left], shapes)
    relation_grad, right_next, right_state_next = put(False, other, relation_grad, [new_right, other_right], shapes)
    return left_next.T, left_state_next[0], right_next.T, right_state_next[0], relation_grad.T


def solution(mesh):
    in_specs = (
        P("dom", None),
        P("dom"),
        P("dom", None),
        P("dom"),
        P(),
        P("dom", "rep"),
        P("dom", "rep"),
        P("dom", "rep"),
        P("dom", "rep", None),
        P("dom", "rep", None),
        P("dom"),
    )
    out_specs = (P("dom", None), P("dom"), P("dom", None), P("dom"), P())
    return jax.shard_map(body, mesh=mesh, in_specs=in_specs, out_specs=out_specs, check_vma=False)
```

```python
import functools

import jax
import jax.numpy as jnp
from jax import lax
from jax.sharding import PartitionSpec as P
from jax.experimental import pallas as pl
from jax.experimental.pallas import tpu as pltpu

MARGIN = 0.1
LEARN_RATE = 0.1
F32 = jnp.float32
BF16 = jnp.bfloat16
NN = (((1,), (0,)), ((), ()))
NT = (((1,), (1,)), ((), ()))


def parts(value):
    high = value.astype(BF16)
    return high, (value - high.astype(F32)).astype(BF16)


def dot(a, b, dims):
    return lax.dot_general(a, b, dims, preferred_element_type=F32)


def dot_picked(value, picks, dims):
    rows = value.shape[0]
    both = dot(jnp.concatenate(parts(value), axis=0), picks, dims)
    return both[:rows] + both[rows:]


def dot_split(a, b, dims):
    rows = a[0].shape[0]
    both = dot(jnp.concatenate(a, axis=0), b[0], dims)
    return both[:rows] + (dot(a[0], b[1], dims) + both[rows:])


def product(v, w):
    return v[0] * w[0] - v[1] * w[1], v[0] * w[1] + v[1] * w[0]


def adjoint(v, w):
    return v[0] * w[0] + v[1] * w[1], v[1] * w[0] - v[0] * w[1]


def halves(x):
    half = x.shape[0] // 2
    return x[:half], x[half:]


def one_hot(ids, rows):
    return (lax.broadcasted_iota(jnp.int32, (rows, ids.shape[1]), 0) == ids).astype(F32)


CORES, X_SIZE, Y_SIZE, Z_SIZE = 2, 4, 4, 8
DEVICES = CORES * X_SIZE * Y_SIZE * Z_SIZE
LANES = 128
VMEM_LIMIT = 32 * 1024 * 1024
COST = 16 * 1024 * 1024


def place(dom, rep):
    return rep % 2, dom // 16, (rep // 2) * 2 + (dom // 8) % 2, dom % 8


def here():
    return place(lax.axis_index("dom"), lax.axis_index("rep"))


def device(core, x, y, z):
    return ((x * 2 + y % 2) * 8 + z) * 4 + (y // 2) * 2 + core


def send(value, target):
    pairs = []
    for n in range(DEVICES):
        pairs.append((n, device(*target(*place(n // 4, n % 4)))))
    return lax.ppermute(value, ("dom", "rep"), pairs)


def to_core(value):
    return send(value, lambda core, x, y, z: (1 - core, x, y, z))


def to_first(value, step):
    return send(
        value,
        lambda core, x, y, z: (core, x, (y + step) % Y_SIZE, z) if core else (core, (x + step) % X_SIZE, y, z),
    )


def to_second(value, step):
    return send(
        value,
        lambda core, x, y, z: (core, (x + step) % X_SIZE, y, z) if core else (core, x, (y + step) % Y_SIZE, z),
    )


def to_y(value, step):
    return send(value, lambda core, x, y, z: (core, x, (y + step) % Y_SIZE, z))


def to_z(value, target):
    return send(value, lambda core, x, y, z: (core, x, y, target(z) % Z_SIZE))


def to_bucket_before(value):
    pairs = []
    for n in range(DEVICES):
        pairs.append((n, (n - 4) % DEVICES))
    return lax.ppermute(value, ("dom", "rep"), pairs)


def piece_rows(total):
    block = total // LANES // (CORES * X_SIZE)
    piece = -(-block // (8 * Y_SIZE)) * 8
    return block, piece


def block_spans(width, types, parity):
    block, piece = piece_rows(width * types)
    found = []
    for k, start, size, row in spans(width, types):
        if row // (piece * Y_SIZE) == parity:
            found.append((k, start, size, row))
    return found


def spans(width, types):
    block, piece = piece_rows(width * types)
    pad = piece * Y_SIZE - block
    found = []
    for k in range(types // LANES):
        row, end = k * width, (k + 1) * width
        while row < end:
            stop = min(end, (row // block + 1) * block)
            found.append((k, row - k * width, stop - row, row + (row // block) * pad))
            row = stop
    return found


def piece_at(half, x, y, r, s, piece):
    first, second = jnp.where(half == 0, x, y), jnp.where(half == 0, y, x)
    return pl.multiple_of(((first + r) % X_SIZE * Y_SIZE + (second + s) % Y_SIZE) * piece, 8)


def grad_kernel(counts_ref, *refs):
    far_refs, near_refs, sems = refs[:8], refs[-9:-1], refs[-1]
    dw_ref, pick_ref, q_ref, p_ref, gr_ref, gl_ref, ds_ref, dt_ref = refs[8:-9]
    fetches = []
    for n, (far_ref, near_ref) in enumerate(zip(far_refs, near_refs)):
        fetches.append(pltpu.make_async_copy(far_ref, near_ref, sems.at[n]))
    for fetch in fetches:
        fetch.start()
    src_ref, rid_ref, dst_ref, negl_ref, negr_ref, near_left_ref, near_right_ref, near_rel_ref = near_refs
    left_ref, right_ref, rel_ref = near_left_ref, near_right_ref, near_rel_ref
    slots = src_ref.shape[1]
    rows = left_ref.shape[1]
    types = rel_ref.shape[1]
    negatives = negl_ref.shape[1]
    for fetch in fetches[:5]:
        fetch.wait()
    pick_src = one_hot(src_ref[...], rows).astype(BF16)
    pick_dst = one_hot(dst_ref[...], rows).astype(BF16)
    pick_rel = one_hot(rid_ref[...], types).astype(BF16)
    fetches[5].wait()
    left = near_left_ref[...]
    source = dot_picked(left, pick_src, NN)
    left_parts, left_rows = parts(left), parts(left.T)
    fetches[6].wait()
    right = near_right_ref[...]
    target = dot_picked(right, pick_dst, NN)
    right_parts, right_rows = parts(right), parts(right.T)
    fetches[7].wait()
    weight = dot_picked(near_rel_ref[...], pick_rel, NN)
    count_right = jnp.sum(one_hot(negr_ref[...], rows), axis=1, keepdims=True)
    count_left = jnp.sum(one_hot(negl_ref[...], rows), axis=1, keepdims=True)
    s, t, w = halves(source), halves(target), halves(weight)
    q = jnp.concatenate(product(s, w), axis=0)
    p = jnp.concatenate(adjoint(t, w), axis=0)
    positive = jnp.sum(q * target, axis=0, keepdims=True)
    q_parts, p_parts = parts(q), parts(p)
    slot = lax.broadcasted_iota(jnp.int32, (1, slots), 1)
    live = (slot + lax.axis_index("rep") * slots < counts_ref[0]).astype(F32) * (1.0 / negatives)
    offset = MARGIN - positive
    g_right = jax.nn.sigmoid(offset + dot_split(right_rows, q_parts, NN)) * count_right * live
    g_left = jax.nn.sigmoid(offset + dot_split(left_rows, p_parts, NN)) * count_left * live
    d_pos = -(jnp.sum(g_right, axis=0, keepdims=True) + jnp.sum(g_left, axis=0, keepdims=True))
    gr_parts, gl_parts = parts(g_right), parts(g_left)
    d_q = dot_split(right_parts, gr_parts, NN) + d_pos * target
    d_p = dot_split(left_parts, gl_parts, NN)
    dq, dp = halves(d_q), halves(d_p)
    a, b = adjoint(dq, s), adjoint(dp, t)
    d_w = jnp.concatenate([a[0] + b[0], a[1] - b[1]], axis=0)
    dw_ref[...], pick_ref[...] = d_w, pick_rel
    q_ref[...], p_ref[...] = q, p
    gr_ref[...], gl_ref[...] = g_right, g_left
    ds_ref[...] = jnp.concatenate(adjoint(dq, w), axis=0)
    dt_ref[...] = jnp.concatenate(product(dp, w), axis=0) + d_pos * q


def blocks_kernel(mine, dw_ref, pick_ref, *refs):
    out_refs, rows_ref = refs[:-1], refs[-1]
    core, x, y, _ = here()
    half = core if mine else 1 - core
    width, types = dw_ref.shape[0], pick_ref.shape[0] // CORES
    block, piece = piece_rows(width * types * CORES)
    pad = piece * Y_SIZE - block
    picks = pick_ref[pl.ds(pl.multiple_of(half * types, LANES), types), :]
    grad = dot_picked(dw_ref[...], picks, NT)
    if pad:
        for k in range(X_SIZE):
            rows_ref[(k + 1) * (block + pad) - pad:(k + 1) * (block + pad), :] = jnp.zeros((pad, LANES), F32)
    for k, start, size, row in spans(width, types * CORES):
        if k < types // LANES:
            rows_ref[row:row + size, :] = grad[start:start + size, k * LANES:(k + 1) * LANES]
    for r, out_ref in enumerate(out_refs):
        for s in range(Y_SIZE):
            at = piece_at(half, x, y, r, s, piece)
            out_ref[s * piece:(s + 1) * piece, :] = rows_ref[pl.ds(at, piece), :]


def rows_kernel(src_ref, dst_ref, q_ref, p_ref, gr_ref, gl_ref, ds_ref, dt_ref, send_ref, keep_ref):
    width = q_ref.shape[0]
    rows = gr_ref.shape[0]
    half = rows // CORES
    first = here()[0] == 0
    for at, ids_ref, edge_ref, score_ref, picked_ref in (
        (0, src_ref, p_ref, gl_ref, ds_ref),
        (width, dst_ref, q_ref, gr_ref, dt_ref),
    ):
        picks = one_hot(ids_ref[...], rows).astype(BF16)
        grad = dot_split(parts(edge_ref[...]), parts(score_ref[...]), NT) + dot_picked(picked_ref[...], picks, NT)
        low, high = grad[:, :half], grad[:, half:]
        keep_ref[at:at + width, :] = jnp.where(first, low, high)
        send_ref[at:at + width, :] = jnp.where(first, high, low)


WHOLE = pl.BlockSpec(memory_space=pltpu.VMEM)


def near(value):
    return pltpu.with_memory_space_constraint(value, pltpu.VMEM)


def far(value):
    return pltpu.with_memory_space_constraint(value, pltpu.HBM)


def call(kernel, specs, arrays, shapes, scratch=(), cost=COST):
    return pl.pallas_call(
        kernel,
        out_shape=[pltpu.VMEM(shape[0], shape[1]) if isinstance(shape[0], tuple) else pltpu.VMEM(shape, F32) for shape in shapes],
        in_specs=list(specs) + [WHOLE] * (len(arrays) - len(specs)),
        out_specs=[WHOLE] * len(shapes),
        scratch_shapes=list(scratch),
        compiler_params=pltpu.CompilerParams(vmem_limit_bytes=VMEM_LIMIT),
        cost_estimate=pl.CostEstimate(flops=0, transcendentals=0, bytes_accessed=cost),
    )(*arrays)


def adagrad_kernel(kept_ref, got_ref, left_ref, right_ref, left_state_ref, right_state_ref, new_left_ref, new_right_ref):
    width = left_ref.shape[0]
    first = here()[0] == 0
    for at, rows_ref, state_ref, out_ref in (
        (0, left_ref, left_state_ref, new_left_ref),
        (width, right_ref, right_state_ref, new_right_ref),
    ):
        half = rows_ref.shape[1] // CORES
        gradient = kept_ref[at:at + width, :] + got_ref[at:at + width, :]
        embedding = jnp.where(first, rows_ref[:, :half], rows_ref[:, half:])
        state = jnp.where(first, state_ref[:, :half], state_ref[:, half:])
        new_state = state + jnp.sum(gradient * gradient, axis=0, keepdims=True) * (1.0 / width)
        out_ref[:width, :] = embedding - gradient * (LEARN_RATE / jnp.sqrt(new_state))
        out_ref[width:, :] = jnp.broadcast_to(new_state, (8, half))


def place_kernel(mine, *refs):
    in_refs, (out_ref, new_rows_ref, new_state_ref) = refs[-X_SIZE - 9:-7], refs[-7:-4]
    rows_ref, joined_ref, state_ref, sems = refs[-4:]
    blocks, (own_ref, other_ref) = in_refs[:X_SIZE], in_refs[X_SIZE:]
    core, x, y, _ = here()
    half = core if mine else 1 - core
    width, types = out_ref.shape
    block, piece = piece_rows(width * types)
    lanes_each = block * LANES // width
    mine_first, mine_second = jnp.where(half == 0, x, y), jnp.where(half == 0, y, x)
    columns = own_ref.shape[1]
    own, other = own_ref[...], other_ref[...]
    for at, value in ((0, jnp.where(core == 0, own, other)), (columns, jnp.where(core == 0, other, own))):
        joined_ref[:, at:at + columns] = value[:width]
        state_ref[:, at:at + columns] = value[width:width + 1]
    copies = [
        pltpu.make_async_copy(joined_ref, new_rows_ref, sems.at[X_SIZE, 0]),
        pltpu.make_async_copy(state_ref, new_state_ref, sems.at[X_SIZE, 1]),
    ]
    for copy in copies:
        copy.start()

    def move(n, begin):
        first = (mine_first + n) % X_SIZE
        for low in range(2):

            @pl.when(first % 2 == low)
            def _():
                at = 0
                for i, (k, start, size, _) in enumerate(block_spans(width, types, low)):
                    lane = (half * X_SIZE + first - low) * lanes_each + k * LANES
                    copy = pltpu.make_async_copy(
                        rows_ref.at[n, pl.ds(at, size), :],
                        out_ref.at[pl.ds(start, size), pl.ds(pl.multiple_of(lane, LANES), LANES)],
                        sems.at[n, i],
                    )
                    if begin:
                        copy.start()
                    else:
                        copy.wait()
                    at += size

    for n, in_ref in enumerate(blocks):
        for s in range(Y_SIZE):
            to = pl.multiple_of((mine_second + s) % Y_SIZE * piece, 8)
            rows_ref[n, pl.ds(to, piece), :] = in_ref[s * piece:(s + 1) * piece, :]
        move(n, True)
    for n in range(X_SIZE):
        move(n, False)
    for copy in copies:
        copy.wait()


def put(mine, blocks, sofar, rows, shapes):
    width, types = shapes[0]
    piece = piece_rows(width * types)[1]
    anywhere = pl.BlockSpec(memory_space=pl.ANY)
    before = [] if sofar is None else [sofar]
    return pl.pallas_call(
        functools.partial(place_kernel, mine),
        out_shape=[jax.ShapeDtypeStruct(shape, F32) for shape in shapes],
        in_specs=[anywhere] * len(before) + [WHOLE] * (X_SIZE + 2),
        out_specs=[anywhere] * 3,
        scratch_shapes=[
            pltpu.VMEM((X_SIZE, piece * Y_SIZE, LANES), F32),
            pltpu.VMEM(shapes[1], F32),
            pltpu.VMEM(shapes[2], F32),
            pltpu.SemaphoreType.DMA((X_SIZE + 1, 2)),
        ],
        input_output_aliases={0: 0} if before else {},
        compiler_params=pltpu.CompilerParams(vmem_limit_bytes=VMEM_LIMIT),
        cost_estimate=pl.CostEstimate(flops=0, transcendentals=0, bytes_accessed=COST),
    )(*before, *[near(value) for value in list(blocks) + list(rows)])


def scatter(pieces, move):
    return sum([move(pieces[r], r) for r in (2, 1, 3)], pieces[0])


def gather(own, count, move):
    got = {r: move(own, (count - r) % count) for r in (2, 3, 1)}
    return [own] + [got[r] for r in range(1, count)]


def after(value, *others):
    return lax.optimization_barrier((value, *others))


def body(left_embedding, left_state, right_embedding, right_state, relation, sources, relation_ids, destinations, negatives_left, negatives_right, edge_counts):
    left, right, relation = left_embedding.T, right_embedding.T, relation.T
    width, types = relation.shape
    rows = left.shape[1]
    edges = sources.shape[1]
    piece = piece_rows(width * types)[1]
    block = (piece * Y_SIZE, LANES)
    scalar = pl.BlockSpec(memory_space=pltpu.SMEM)
    given = (sources, relation_ids, destinations, negatives_left[0], negatives_right[0], left, right, relation)
    found = call(
        grad_kernel,
        [scalar] + [pl.BlockSpec(memory_space=pl.ANY)] * len(given),
        [edge_counts] + [far(value) for value in given],
        [(width, edges), ((types, edges), BF16)] + [(width, edges)] * 2 + [(rows, edges)] * 2 + [(width, edges)] * 2,
        [pltpu.VMEM(value.shape, value.dtype) for value in given] + [pltpu.SemaphoreType.DMA((len(given),))],
    )
    by_relation, saved = [near(value) for value in found[:2]], found[2:]
    staging = [pltpu.VMEM((X_SIZE * block[0], LANES), F32)]
    rel_send = call(functools.partial(blocks_kernel, False), [], by_relation, [block] * X_SIZE, staging)
    rel_keep = call(functools.partial(blocks_kernel, True), [], by_relation, [block] * X_SIZE, staging)

    blocks = {}
    for r in (2, 1, 3, 0):
        blocks[r] = rel_keep[r] + to_core(rel_send[r])
    blocks[3], *saved = after(blocks[3], *saved)
    mine = scatter([blocks[r] for r in range(X_SIZE)], to_first)

    lr_half = (2 * width, rows // CORES)
    lr_send, lr_keep = call(rows_kernel, [], [far(sources), far(destinations)] + [near(value) for value in saved], [lr_half, lr_half])
    lr_sum = lr_keep + to_core(lr_send)

    pieces = []
    for r in range(Y_SIZE):
        pieces.append(mine[r * piece:(r + 1) * piece])
    mine = scatter(pieces, to_second)

    mine = mine + to_z(mine, lambda z: z ^ 1)
    mine, lr_sum = after(mine, lr_sum)
    lr_other = to_y(lr_sum, 2)
    opposite = to_z(mine, lambda z: z ^ 5)
    nearer = to_z(mine, lambda z: z + 1 if z % 2 else z - 1)
    other_side = to_z(mine, lambda z: z + 2 if z % 2 else z - 2)
    mine = (mine + opposite) + (nearer + other_side)
    found = gather(mine, Y_SIZE, to_second)
    found[2], lr_sum, lr_other = after(found[2], lr_sum, lr_other)
    packed = (width + 8, rows // CORES)
    new_left, new_right = call(
        adagrad_kernel,
        [],
        [near(lr_sum), near(lr_other)] + [far(value) for value in (left, right, left_state[None], right_state[None])],
        [packed, packed],
        cost=0,
    )
    *found, new_left, new_right = after(*found, new_left, new_right)
    new_right = to_bucket_before(new_right)
    other_left = to_core(new_left)
    *found, other_left = after(*found, other_left)
    own = gather(jnp.concatenate(found, axis=0), X_SIZE, to_first)
    other_right = to_core(new_right)
    other = [to_core(value) for value in own]
    shapes = [(width, types), (width, rows), (1, rows)]
    relation_grad, left_next, left_state_next = put(True, own, None, [new_left, other_left], shapes)
    relation_grad, right_next, right_state_next = put(False, other, relation_grad, [new_right, other_right], shapes)
    return left_next.T, left_state_next[0], right_next.T, right_state_next[0], relation_grad.T


def solution(mesh):
    in_specs = (
        P("dom", None),
        P("dom"),
        P("dom", None),
        P("dom"),
        P(),
        P("dom", "rep"),
        P("dom", "rep"),
        P("dom", "rep"),
        P("dom", "rep", None),
        P("dom", "rep", None),
        P("dom"),
    )
    out_specs = (P("dom", None), P("dom"), P("dom", None), P("dom"), P())
    return jax.shard_map(body, mesh=mesh, in_specs=in_specs, out_specs=out_specs, check_vma=False)
```
